128 devices in a mesh: comp: 2 (over z_lo), tile: 64 (over z_hi, x, y, core).
Axes of the slice: x: 4, y: 4, z: 4 (z_hi: 2, z_lo: 2; z = z_hi * 2 + z_lo), core: 2. Of those that a mesh axis runs over, the one named last changes fastest.
Arguments:
- state: float32 [2, 16, 2048, 256], P('comp', None, 'tile'), may hold values from -6 to 6
- weights: bfloat16 [2, 4096, 4, 128, 128], P('comp', 'tile'), may hold values from -0.25 to 0.25
- send_slots: int32 [2, 64, 64, 8], P('comp', 'tile'), may hold values from 0 to 63, as said below
- recv_pos: int32 [2, 4096, 4], P('comp', 'tile'), may hold values from 0 to 511, as said below
- diffusion: float32 [2, 16], P('comp'), may hold values from 0.02 to 0.24
- coupling: float32 [2, 16], P('comp'), may hold values from 0.2 to 1
- sea_mask: int32 [2048, 256], P('tile'), may hold values 0 or 1
Outputs:
- new_state: float32 [2, 16, 2048, 256], P('comp', None, 'tile')
- incoming: float32 [2, 16, 2048, 256], P('comp', None, 'tile')
The draws below stay inside these ranges and needn't reach their ends.
Inputs may be any that keep to these rules, and one draw needn't show every extreme that they name: `send_slots`: the block of tile s carried in slot j from tile s to tile t for component c's needs. `recv_pos`: slot positions source tile times 8 plus j, all different within one receiving tile; in every receiving tile one source tile fills all its 8 slots.
All inputs are finite; a program needn't handle non-finite values. No bound on the sum of `sea_mask` on one device may be relied on, other than what follows from the above.
Results may differ from the reference program's by a relative error of at most 0.0029.
Values may be sent and summed in bfloat16 or wider, within the bound.
A program may use at most 128 MiB of HBM per device.

```python
import math
import jax
import jax.numpy as jnp

FIELDS = 16
ROWS_DEV = 32
COLUMNS = 256
BLOCK = 128
SOURCES = 4
BLOCKS_DEV = 64
TILES = 64
SLOTS = 8


def plan_lists(key):
    key_first = jax.random.fold_in(key, 11)
    key_perm = jax.random.fold_in(key, 12)
    key_slot = jax.random.fold_in(key, 13)
    key_mix = jax.random.fold_in(key, 14)
    sends = jax.random.randint(key_slot, (2, TILES, TILES, SLOTS), 0, BLOCKS_DEV).astype(jnp.int32)
    firsts = jax.random.randint(key_first, (2, TILES), 0, TILES).astype(jnp.int32)
    perm_keys = jax.random.split(key_perm, 2 * TILES)
    perms = jax.vmap(lambda k: jax.random.permutation(k, TILES * SLOTS))(perm_keys).astype(jnp.int32)
    perms = perms.reshape(2, TILES, TILES * SLOTS)
    groups = (jnp.arange(TILES * SLOTS) // SLOTS).astype(jnp.int32)
    scores = perms + TILES * SLOTS * (groups[None, None, :] == firsts[:, :, None]).astype(jnp.int32)
    order = jnp.argsort(-scores, axis=-1).astype(jnp.int32)
    chosen = order[:, :, :BLOCKS_DEV * SOURCES]
    mix_keys = jax.random.split(key_mix, 2 * TILES)
    mixes = jax.vmap(lambda k: jax.random.permutation(k, BLOCKS_DEV * SOURCES))(mix_keys).astype(jnp.int32)
    mixes = mixes.reshape(2, TILES, BLOCKS_DEV * SOURCES)
    chosen = jnp.take_along_axis(chosen, mixes, axis=-1)
    return (sends, chosen.reshape(2, TILES * BLOCKS_DEV, SOURCES))


def draw_send_slots(key, part):
    return plan_lists(key)[0]


def draw_recv_pos(key, part):
    return plan_lists(key)[1]


def plant(values, own_key, low, top_value):
    longest = values.shape.index(max(values.shape))
    spots = []
    for shift in (0, 1):
        where = [jax.random.randint(jax.random.fold_in(own_key, axis), (), 0, length) for axis, length in enumerate(values.shape)]
        where[longest] = (where[longest] + shift) % values.shape[longest]
        spots.append(tuple(where))
    return values.at[spots[0]].set(low).at[spots[1]].set(top_value)


def shard_levels(rng, dims, shards, least, high):
    level = 1.0
    for dim, shards_of in shards:
        draws = jax.random.uniform(jax.random.fold_in(jax.random.fold_in(rng, 6), dim), (shards_of,), jnp.float32, least / len(shards), high / len(shards))
        level = level * jnp.repeat(jnp.exp(draws), dims[dim] // shards_of).reshape((-1,) + (1,) * (len(dims) - 1 - dim))
    return level


def gaussian(rng, dims, width, most, shards=(), dtype=jnp.bfloat16):
    result = width * jax.random.normal(rng, dims, jnp.float32)
    if shards:
        result = result * shard_levels(rng, dims, shards, -0.22, 0.18)
    return jnp.clip(result, -most, most).astype(dtype)


def setup_inputs(seed: int = 0) -> dict:
    streams_of = jax.random.split(jax.random.key(seed), 8)
    return {
        "state": gaussian(streams_of[0], (2, FIELDS, TILES * ROWS_DEV, COLUMNS), 1.0, 6.0, ((0, 2), (2, 64)), jnp.float32),
        "weights": gaussian(streams_of[1], (2, TILES * BLOCKS_DEV, SOURCES, BLOCK, BLOCK), (SOURCES * BLOCK) ** -0.5, 0.25, ((0, 2), (1, 64))),
        "send_slots": draw_send_slots(jax.random.fold_in(streams_of[7], 71), 0),
        "recv_pos": draw_recv_pos(jax.random.fold_in(streams_of[7], 71), 0),
        "diffusion": jnp.clip(jnp.exp(math.log(0.24) - 2.4849066 * jax.random.uniform(streams_of[4], (2, FIELDS), jnp.float32) ** shard_levels(streams_of[4], (2, FIELDS), ((0, 2),), -0.2, 0.2)), 0.02, 0.24),
        "coupling": jnp.clip(0.2 + 0.8 * jax.random.uniform(streams_of[5], (2, FIELDS), jnp.float32) ** shard_levels(streams_of[5], (2, FIELDS), ((0, 2),), -0.2, 0.2), 0.2, 1.0),
        "sea_mask": plant((jax.random.randint(streams_of[6], (TILES * ROWS_DEV, COLUMNS), 0, 4) < 3).astype(jnp.int32), jax.random.fold_in(streams_of[6], 1), 0, 1),
    }


def step_field(field, rates, cover):
    for substep in range(2):
        laplace = jnp.roll(field, 1, 1) + jnp.roll(field, -1, 1) + jnp.roll(field, 1, 2) + jnp.roll(field, -1, 2) - 4.0 * field
        field = field + rates[:, None, None] * cover * laplace
    return field


def reference(state, weights, send_slots, recv_pos, diffusion, coupling, sea_mask):
    surface = state.astype(jnp.bfloat16).reshape(2, FIELDS, TILES * BLOCKS_DEV, BLOCK)
    dest_tile = (jnp.arange(TILES * BLOCKS_DEV) // BLOCKS_DEV).astype(jnp.int32)
    results = []
    arrivals = []
    for comp in range(2):
        position = recv_pos[comp]
        src_tile = position // SLOTS
        slot_index = position % SLOTS
        source = src_tile * BLOCKS_DEV + send_slots[comp][src_tile, dest_tile[:, None], slot_index]
        picked = surface[1 - comp][:, source, :].astype(jnp.float32)
        flux = jnp.einsum('vbkc,bkdc->vbd', picked, weights[comp].astype(jnp.float32))
        flux = flux.reshape(FIELDS, TILES * ROWS_DEV, COLUMNS)
        if comp == 1:
            cover = sea_mask.astype(jnp.float32)
        else:
            cover = jnp.ones((TILES * ROWS_DEV, COLUMNS), jnp.float32)
        stepped = step_field(state[comp], diffusion[comp], cover)
        results.append(stepped + coupling[comp][:, None, None] * cover * flux)
        arrivals.append(flux)
    return jnp.stack(results), jnp.stack(arrivals)
```

```python
import functools

import jax
import jax.numpy as jnp
from jax import lax
from jax.experimental import pallas as pl
from jax.experimental.pallas import tpu as pltpu
from jax.sharding import PartitionSpec as P

BLOCK = 128
MESH = pl.DeviceIdType.MESH


def target_tile(me, step, tiles):
    if tiles != 64:
        return lax.rem(me + step, tiles)
    core = (me % 2 + step % 2) % 2
    z_hi = (me // 32 + step // 2) % 2
    x = (me // 8 % 4 + step // 4) % 4
    y = (me // 2 % 4 + step // 16) % 4
    return z_hi * 32 + x * 8 + y * 2 + core


def kernel(
    tiles, slots, fields, rows, columns, blocks, sources,
    state_hbm, weights_hbm, lists_hbm, pos_hbm, diffusion_hbm, coupling_hbm, mask_hbm,
    new_ref, flux_ref,
    lists_ref, pos_ref, diffusion_ref, coupling_ref, mask_ref, cells, weights, surface, lists_v, lists_s, outbox, inbox, cover, edge, halo, side, stepped, flux,
    small_sem, state_sem, weights_sem, lists_sem, edge_send, edge_recv, list_send, list_recv, box_send, box_recv,
):
    comp, me = lax.axis_index("comp"), lax.axis_index("tile")
    other = 1 - comp
    above, below = (me + tiles - 1) % tiles, (me + 1) % tiles
    halves = columns // BLOCK

    load_state = [
        pltpu.make_async_copy(
            state_hbm.at[:, pl.ds(half * BLOCK, BLOCK)], cells.at[half], state_sem.at[half]
        )
        for half in range(halves)
    ]
    for copy in load_state:
        copy.start()
    load_small = [
        pltpu.make_async_copy(source, target, small_sem.at[number])
        for number, (source, target) in enumerate((
            (lists_hbm, lists_ref), (pos_hbm, pos_ref), (diffusion_hbm, diffusion_ref),
            (coupling_hbm, coupling_ref), (mask_hbm, mask_ref),
        ))
    ]
    for copy in load_small:
        copy.start()
    load_weights = pltpu.make_async_copy(weights_hbm, weights, weights_sem)
    load_weights.start()

    barrier = pltpu.get_barrier_semaphore()
    for neighbour in (above, below):
        pl.semaphore_signal(barrier, inc=1, device_id=(comp, neighbour), device_id_type=MESH)

    @pl.loop(0, tiles)
    def _(step):
        pl.semaphore_signal(
            barrier, inc=1, device_id=(other, target_tile(me, step, tiles)), device_id_type=MESH
        )

    for copy in load_small:
        copy.wait()
    cover[...] = jnp.where(comp == 1, mask_ref[...].astype(jnp.float32), 1.0)
    for copy in load_state:
        copy.wait()

    @pl.loop(0, rows)
    def _(row):
        for half in range(halves):
            picked = cells[half, pl.ds(row, fields, stride=rows)]
            surface[row * halves + half] = picked.astype(jnp.bfloat16)

    def whole(ref, here):
        return jnp.concatenate([ref[half, here] for half in range(halves)], axis=1)

    def line(row):
        return whole(cells, pl.ds(row, fields, stride=rows))

    edge[0, 0:fields] = line(0)
    edge[0, fields:2 * fields] = line(1)
    edge[0, 2 * fields:] = jnp.broadcast_to(cover[0:1], (8, columns))
    edge[1, 0:fields] = line(rows - 1)
    edge[1, fields:2 * fields] = line(rows - 2)
    edge[1, 2 * fields:] = jnp.broadcast_to(cover[rows - 1:rows], (8, columns))

    pl.semaphore_wait(barrier, tiles + 2)

    send_lists = pltpu.make_async_remote_copy(
        src_ref=lists_ref, dst_ref=lists_v, send_sem=list_send, recv_sem=list_recv,
        device_id=(other, me), device_id_type=MESH,
    )
    send_lists.start()
    send_edges = [
        pltpu.make_async_remote_copy(
            src_ref=edge.at[end], dst_ref=halo.at[end], send_sem=edge_send.at[end],
            recv_sem=edge_recv.at[end], device_id=(comp, neighbour), device_id_type=MESH,
        )
        for end, neighbour in ((0, above), (1, below))
    ]
    for copy in send_edges:
        copy.start()
    send_lists.wait()
    move_lists = pltpu.make_async_copy(lists_v, lists_s, lists_sem)
    move_lists.start()
    move_lists.wait()

    @pl.loop(0, tiles)
    def _(step):
        tile = target_tile(me, step, tiles)
        for slot in range(slots):
            outbox[tile, slot] = surface[lists_s[slot, tile]]
        pltpu.make_async_remote_copy(
            src_ref=outbox.at[tile], dst_ref=inbox.at[pl.ds(me * slots, slots)],
            send_sem=box_send, recv_sem=box_recv,
            device_id=(other, tile), device_id_type=MESH,
        ).start()

    for copy in send_edges:
        copy.wait()
    number = lax.broadcasted_iota(jnp.int32, (fields, columns), 0)
    rates = jnp.zeros((fields, columns), jnp.float32)
    for field in range(fields):
        rates = jnp.where(number == field, diffusion_ref[0, field], rates)

    def across(value):
        return pltpu.roll(value, 1, 1) + pltpu.roll(value, columns - 1, 1)

    for end, row in ((1, 0), (0, rows - 1)):
        near, far = halo[end, 0:fields], halo[end, fields:2 * fields]
        total = far + line(row) + across(near) - 4.0 * near
        side[end] = near + rates * halo[end, 2 * fields:2 * fields + 1] * total

    row_number = lax.broadcasted_iota(jnp.int32, (rows, columns), 0)

    def substep(value, first, last, rate):
        up = jnp.where(row_number == 0, first, pltpu.roll(value, 1, 0))
        down = jnp.where(row_number == rows - 1, last, pltpu.roll(value, rows - 1, 0))
        total = up + down + across(value) - 4.0 * value
        return value + rate * cover[...] * total

    @pl.loop(0, fields)
    def _(field):
        here = pl.ds(pl.multiple_of(field * rows, rows), rows)
        rate = diffusion_ref[0, field]
        value = whole(cells, here)
        value = substep(value, halo[1, pl.ds(field, 1)], halo[0, pl.ds(field, 1)], rate)
        value = substep(value, side[1, pl.ds(field, 1)], side[0, pl.ds(field, 1)], rate)
        stepped[here] = value

    load_weights.wait()
    pltpu.make_async_copy(inbox, inbox, box_recv).wait()

    @pl.loop(0, blocks // halves)
    def _(row):
        for half in range(halves):
            block = row * halves + half
            total = jnp.zeros((fields, BLOCK), jnp.float32)
            for source in range(sources):
                total += lax.dot_general(
                    inbox[pos_ref[source, block]], weights[block, source],
                    (((1,), (1,)), ((), ())), preferred_element_type=jnp.float32,
                )
            flux[half, pl.ds(row, fields, stride=rows)] = total

    @pl.loop(0, fields)
    def _(field):
        here = pl.ds(pl.multiple_of(field * rows, rows), rows)
        arrived = whole(flux, here)
        flux_ref[here] = arrived
        new_ref[here] = stepped[here] + coupling_ref[0, field] * cover[...] * arrived

    pltpu.make_async_copy(outbox, outbox, box_send).wait()


def per_device(tiles, state, weights, send_slots, recv_pos, diffusion, coupling, sea_mask):
    _, fields, rows, columns = state.shape
    blocks, sources = recv_pos.shape[1:]
    slots = send_slots.shape[3]
    lists = send_slots[0, 0].T
    positions = recv_pos[0].T
    flat = jax.ShapeDtypeStruct((fields * rows, columns), jnp.float32)
    vmem, hbm = pl.BlockSpec(memory_space=pltpu.VMEM), pl.BlockSpec(memory_space=pltpu.HBM)
    edge_rows = 2 * fields + 8
    dma = pltpu.SemaphoreType.DMA
    new, flux = pl.pallas_call(
        functools.partial(kernel, tiles, slots, fields, rows, columns, blocks, sources),
        out_shape=(flat, flat),
        in_specs=[hbm] * 7,
        out_specs=(vmem, vmem),
        scratch_shapes=[
            pltpu.VMEM((slots, tiles), jnp.int32),
            pltpu.SMEM((sources, blocks), jnp.int32),
            pltpu.SMEM((1, fields), jnp.float32),
            pltpu.SMEM((1, fields), jnp.float32),
            pltpu.VMEM((rows, columns), jnp.int32),
            pltpu.VMEM((columns // BLOCK, fields * rows, BLOCK), jnp.float32),
            pltpu.VMEM((blocks, sources, BLOCK, BLOCK), jnp.bfloat16),
            pltpu.VMEM((blocks, fields, BLOCK), jnp.bfloat16),
            pltpu.VMEM((slots, tiles), jnp.int32),
            pltpu.SMEM((slots, tiles), jnp.int32),
            pltpu.VMEM((tiles, slots, fields, BLOCK), jnp.bfloat16),
            pltpu.VMEM((tiles * slots, fields, BLOCK), jnp.bfloat16),
            pltpu.VMEM((rows, columns), jnp.float32),
            pltpu.VMEM((2, edge_rows, columns), jnp.float32),
            pltpu.VMEM((2, edge_rows, columns), jnp.float32),
            pltpu.VMEM((2, fields, columns), jnp.float32),
            pltpu.VMEM((fields * rows, columns), jnp.float32),
            pltpu.VMEM((columns // BLOCK, fields * rows, BLOCK), jnp.float32),
            dma((5,)), dma((columns // BLOCK,)), dma, dma, dma((2,)), dma((2,)), dma, dma, dma, dma,
        ],
        compiler_params=pltpu.CompilerParams(
            collective_id=0, has_side_effects=True, vmem_limit_bytes=60 * 2**20
        ),
    )(state.reshape(fields * rows, columns), weights[0], lists, positions, diffusion, coupling, sea_mask)
    return new.reshape(state.shape), flux.reshape(state.shape)


def solution(mesh):
    return jax.shard_map(
        functools.partial(per_device, mesh.shape["tile"]),
        mesh=mesh,
        in_specs=(
            P("comp", None, "tile", None),
            P("comp", "tile", None, None, None),
            P("comp", "tile", None, None),
            P("comp", "tile", None),
            P("comp", None),
            P("comp", None),
            P("tile", None),
        ),
        out_specs=(P("comp", None, "tile", None), P("comp", None, "tile", None)),
        check_vma=False,
    )
```

```python
import functools

import jax
import jax.numpy as jnp
from jax import lax
from jax.experimental import pallas as pl
from jax.experimental.pallas import tpu as pltpu
from jax.sharding import PartitionSpec as P

BLOCK = 128
MESH = pl.DeviceIdType.MESH


def target_tile(me, step, tiles):
    if tiles != 64:
        return lax.rem(me + step, tiles)
    x, turn, part = step % 4, step // 4 % 4, step // 16
    y, z_hi, core = (x + turn) % 4, (x + part) % 2, part // 2
    return me ^ (z_hi * 32 + x * 8 + y * 2 + core)


def kernel(
    tiles, slots, fields, rows, columns, blocks, sources,
    state_hbm, weights_hbm, lists_hbm, pos_hbm, diffusion_hbm, coupling_hbm, mask_hbm,
    new_ref, flux_ref,
    pos_ref, diffusion_ref, coupling_ref, mask_ref, cells, weights, surface, lists, outbox, inbox, cover, edge, halo, side, stepped, flux,
    small_sem, state_sem, weights_sem, edge_send, edge_recv, list_send, list_recv, box_send, box_recv,
):
    comp, me = lax.axis_index("comp"), lax.axis_index("tile")
    other = 1 - comp
    above, below = (me + tiles - 1) % tiles, (me + 1) % tiles
    halves = columns // BLOCK

    load_state = [
        pltpu.make_async_copy(
            state_hbm.at[:, pl.ds(half * BLOCK, BLOCK)], cells.at[half], state_sem.at[half]
        )
        for half in range(halves)
    ]
    for copy in load_state:
        copy.start()
    load_small = [
        pltpu.make_async_copy(source, target, small_sem.at[number])
        for number, (source, target) in enumerate((
            (pos_hbm, pos_ref), (diffusion_hbm, diffusion_ref),
            (coupling_hbm, coupling_ref), (mask_hbm, mask_ref),
        ))
    ]
    for copy in load_small:
        copy.start()
    load_weights = pltpu.make_async_copy(weights_hbm, weights, weights_sem)
    load_weights.start()

    barrier = pltpu.get_barrier_semaphore()
    for neighbour in (above, below):
        pl.semaphore_signal(barrier, inc=1, device_id=(comp, neighbour), device_id_type=MESH)

    @pl.loop(0, tiles)
    def _(step):
        pl.semaphore_signal(
            barrier, inc=1, device_id=(other, target_tile(me, step, tiles)), device_id_type=MESH
        )

    for copy in load_small:
        copy.wait()
    cover[...] = jnp.where(comp == 1, mask_ref[...].astype(jnp.float32), 1.0)
    for copy in load_state:
        copy.wait()

    @pl.loop(0, rows)
    def _(row):
        for half in range(halves):
            picked = cells[half, pl.ds(row, fields, stride=rows)]
            surface[row * halves + half] = picked.astype(jnp.bfloat16)

    def whole(ref, here):
        return jnp.concatenate([ref[half, here] for half in range(halves)], axis=1)

    def line(row):
        return whole(cells, pl.ds(row, fields, stride=rows))

    edge[0, 0:fields] = line(0)
    edge[0, fields:2 * fields] = line(1)
    edge[0, 2 * fields:] = jnp.broadcast_to(cover[0:1], (8, columns))
    edge[1, 0:fields] = line(rows - 1)
    edge[1, fields:2 * fields] = line(rows - 2)
    edge[1, 2 * fields:] = jnp.broadcast_to(cover[rows - 1:rows], (8, columns))

    pl.semaphore_wait(barrier, tiles + 2)

    send_lists = pltpu.make_async_remote_copy(
        src_ref=lists_hbm, dst_ref=lists, send_sem=list_send, recv_sem=list_recv,
        device_id=(other, me), device_id_type=MESH,
    )
    send_lists.start()
    send_edges = [
        pltpu.make_async_remote_copy(
            src_ref=edge.at[end], dst_ref=halo.at[end], send_sem=edge_send.at[end],
            recv_sem=edge_recv.at[end], device_id=(comp, neighbour), device_id_type=MESH,
        )
        for end, neighbour in ((0, above), (1, below))
    ]
    for copy in send_edges:
        copy.start()
    send_lists.wait()

    @pl.loop(0, tiles)
    def _(step):
        tile = target_tile(me, step, tiles)
        for slot in range(slots):
            outbox[tile, slot] = surface[lists[slot, tile]]
        pltpu.make_async_remote_copy(
            src_ref=outbox.at[tile], dst_ref=inbox.at[pl.ds(me * slots, slots)],
            send_sem=box_send, recv_sem=box_recv,
            device_id=(other, tile), device_id_type=MESH,
        ).start()

    for copy in send_edges:
        copy.wait()
    number = lax.broadcasted_iota(jnp.int32, (fields, columns), 0)
    rates = jnp.zeros((fields, columns), jnp.float32)
    for field in range(fields):
        rates = jnp.where(number == field, diffusion_ref[0, field], rates)

    def across(value):
        return pltpu.roll(value, 1, 1) + pltpu.roll(value, columns - 1, 1)

    for end, row in ((1, 0), (0, rows - 1)):
        near, far = halo[end, 0:fields], halo[end, fields:2 * fields]
        total = far + line(row) + across(near) - 4.0 * near
        side[end] = near + rates * halo[end, 2 * fields:2 * fields + 1] * total

    row_number = lax.broadcasted_iota(jnp.int32, (rows, columns), 0)

    def substep(value, first, last, rate):
        up = jnp.where(row_number == 0, first, pltpu.roll(value, 1, 0))
        down = jnp.where(row_number == rows - 1, last, pltpu.roll(value, rows - 1, 0))
        total = up + down + across(value) - 4.0 * value
        return value + rate * cover[...] * total

    @pl.loop(0, fields)
    def _(field):
        here = pl.ds(pl.multiple_of(field * rows, rows), rows)
        rate = diffusion_ref[0, field]
        value = whole(cells, here)
        value = substep(value, halo[1, pl.ds(field, 1)], halo[0, pl.ds(field, 1)], rate)
        value = substep(value, side[1, pl.ds(field, 1)], side[0, pl.ds(field, 1)], rate)
        stepped[here] = value

    load_weights.wait()
    pltpu.make_async_copy(inbox, inbox, box_recv).wait()

    @pl.loop(0, blocks // halves, unroll=8)
    def _(row):
        for half in range(halves):
            block = row * halves + half
            picked = jnp.concatenate([inbox[pos_ref[source, block]] for source in range(sources)], axis=1)
            weight = jnp.concatenate([weights[block, source] for source in range(sources)], axis=1)
            flux[half, pl.ds(row, fields, stride=rows)] = lax.dot_general(
                picked, weight, (((1,), (1,)), ((), ())), preferred_element_type=jnp.float32,
            )

    @pl.loop(0, fields)
    def _(field):
        here = pl.ds(pl.multiple_of(field * rows, rows), rows)
        arrived = whole(flux, here)
        flux_ref[here] = arrived
        new_ref[here] = stepped[here] + coupling_ref[0, field] * cover[...] * arrived

    pltpu.make_async_copy(outbox, outbox, box_send).wait()


def per_device(tiles, state, weights, send_slots, recv_pos, diffusion, coupling, sea_mask):
    _, fields, rows, columns = state.shape
    blocks, sources = recv_pos.shape[1:]
    slots = send_slots.shape[3]
    flat = jax.ShapeDtypeStruct((fields * rows, columns), jnp.float32)
    vmem, hbm = pl.BlockSpec(memory_space=pltpu.VMEM), pl.BlockSpec(memory_space=pltpu.HBM)
    edge_rows = 2 * fields + 8
    dma = pltpu.SemaphoreType.DMA
    new, flux = pl.pallas_call(
        functools.partial(kernel, tiles, slots, fields, rows, columns, blocks, sources),
        out_shape=(flat, flat),
        in_specs=[hbm] * 7,
        out_specs=(vmem, vmem),
        scratch_shapes=[
            pltpu.SMEM((sources, blocks), jnp.int32),
            pltpu.SMEM((1, fields), jnp.float32),
            pltpu.SMEM((1, fields), jnp.float32),
            pltpu.VMEM((rows, columns), jnp.int32),
            pltpu.VMEM((columns // BLOCK, fields * rows, BLOCK), jnp.float32),
            pltpu.VMEM((blocks, sources, BLOCK, BLOCK), jnp.bfloat16),
            pltpu.VMEM((blocks, fields, BLOCK), jnp.bfloat16),
            pltpu.SMEM((slots, tiles), jnp.int32),
            pltpu.VMEM((tiles, slots, fields, BLOCK), jnp.bfloat16),
            pltpu.VMEM((tiles * slots, fields, BLOCK), jnp.bfloat16),
            pltpu.VMEM((rows, columns), jnp.float32),
            pltpu.VMEM((2, edge_rows, columns), jnp.float32),
            pltpu.VMEM((2, edge_rows, columns), jnp.float32),
            pltpu.VMEM((2, fields, columns), jnp.float32),
            pltpu.VMEM((fields * rows, columns), jnp.float32),
            pltpu.VMEM((columns // BLOCK, fields * rows, BLOCK), jnp.float32),
            dma((4,)), dma((columns // BLOCK,)), dma, dma((2,)), dma((2,)), dma, dma, dma, dma,
        ],
        compiler_params=pltpu.CompilerParams(
            collective_id=0, has_side_effects=True, vmem_limit_bytes=32 * 2**20
        ),
    )(*(pltpu.with_memory_space_constraint(value, pltpu.HBM) for value in (
        state.reshape(fields * rows, columns), weights[0], send_slots[0, 0].T, recv_pos[0].T, diffusion, coupling, sea_mask
    )))
    return new.reshape(state.shape), flux.reshape(state.shape)


def solution(mesh):
    return jax.shard_map(
        functools.partial(per_device, mesh.shape["tile"]),
        mesh=mesh,
        in_specs=(
            P("comp", None, "tile", None),
            P("comp", "tile", None, None, None),
            P("comp", "tile", None, None),
            P("comp", "tile", None),
            P("comp", None),
            P("comp", None),
            P("tile", None),
        ),
        out_specs=(P("comp", None, "tile", None), P("comp", None, "tile", None)),
        check_vma=False,
    )
```

```python
import functools

import jax
import jax.numpy as jnp
from jax import lax
from jax.experimental import pallas as pl
from jax.experimental.pallas import tpu as pltpu
from jax.sharding import PartitionSpec as P

BLOCK = 128
GROUP = 4
GROUP_ROWS = 8
MESH = pl.DeviceIdType.MESH


def target_tile(me, step, tiles):
    if tiles != 64:
        return lax.rem(me + step, tiles)
    x, turn, part = step % 4, step // 4 % 4, step // 16
    y, z_hi, core = (x + turn) % 4, (x + part) % 2, part // 2
    return me ^ (z_hi * 32 + x * 8 + y * 2 + core)


def exchange(
    tiles, slots, fields, rows, columns, blocks, sources,
    state_hbm, weights_hbm, lists_hbm, pos_hbm, diffusion_hbm, coupling_hbm, mask_hbm,
    products, stepped, cover, gains, pos_ref,
    diffusion_ref, coupling_ref, mask_ref, cells, weights, surface, lists, outbox, inbox, edge, halo, side, users_v, users,
    small_sem, state_sem, weights_sem, users_sem, edge_send, edge_recv, list_send, list_recv, box_send, box_recv,
):
    comp, me = lax.axis_index("comp"), lax.axis_index("tile")
    other = 1 - comp
    above, below = (me + tiles - 1) % tiles, (me + 1) % tiles
    halves = columns // BLOCK

    load_state = [
        pltpu.make_async_copy(
            state_hbm.at[:, pl.ds(half * BLOCK, BLOCK)], cells.at[half], state_sem.at[half]
        )
        for half in range(halves)
    ]
    for copy in load_state:
        copy.start()
    load_small = [
        pltpu.make_async_copy(source, target, small_sem.at[number])
        for number, (source, target) in enumerate((
            (pos_hbm, pos_ref), (diffusion_hbm, diffusion_ref),
            (coupling_hbm, coupling_ref), (mask_hbm, mask_ref),
        ))
    ]
    for copy in load_small:
        copy.start()
    load_weights = pltpu.make_async_copy(weights_hbm, weights, weights_sem)
    load_weights.start()

    barrier = pltpu.get_barrier_semaphore()
    for neighbour in (above, below):
        pl.semaphore_signal(barrier, inc=1, device_id=(comp, neighbour), device_id_type=MESH)

    @pl.loop(0, tiles, unroll=tiles)
    def _(step):
        pl.semaphore_signal(
            barrier, inc=1, device_id=(other, target_tile(me, step, tiles)), device_id_type=MESH
        )

    for copy in load_small:
        copy.wait()
    cover[...] = jnp.where(comp == 1, mask_ref[...].astype(jnp.float32), 1.0)
    for copy in load_state:
        copy.wait()

    @pl.loop(0, rows)
    def _(row):
        for half in range(halves):
            picked = cells[half, pl.ds(row, fields, stride=rows)]
            surface[row * halves + half] = picked.astype(jnp.bfloat16)

    def whole(ref, here):
        return jnp.concatenate([ref[half, here] for half in range(halves)], axis=1)

    def line(row):
        return whole(cells, pl.ds(row, fields, stride=rows))

    edge[0, 0:fields] = line(0)
    edge[0, fields:2 * fields] = line(1)
    edge[0, 2 * fields:] = jnp.broadcast_to(cover[0:1], (8, columns))
    edge[1, 0:fields] = line(rows - 1)
    edge[1, fields:2 * fields] = line(rows - 2)
    edge[1, 2 * fields:] = jnp.broadcast_to(cover[rows - 1:rows], (8, columns))

    pl.semaphore_wait(barrier, tiles + 2)

    send_lists = pltpu.make_async_remote_copy(
        src_ref=lists_hbm, dst_ref=lists, send_sem=list_send, recv_sem=list_recv,
        device_id=(other, me), device_id_type=MESH,
    )
    send_lists.start()
    send_edges = [
        pltpu.make_async_remote_copy(
            src_ref=edge.at[end], dst_ref=halo.at[end], send_sem=edge_send.at[end],
            recv_sem=edge_recv.at[end], device_id=(comp, neighbour), device_id_type=MESH,
        )
        for end, neighbour in ((0, above), (1, below))
    ]
    for copy in send_edges:
        copy.start()
    send_lists.wait()

    @pl.loop(0, tiles, unroll=tiles)
    def _(step):
        tile = target_tile(me, step, tiles)
        for slot in range(slots):
            outbox[tile, slot] = surface[lists[slot, tile]]
        pltpu.make_async_remote_copy(
            src_ref=outbox.at[tile], dst_ref=inbox.at[pl.ds(me * slots, slots)],
            send_sem=box_send, recv_sem=box_recv.at[me],
            device_id=(other, tile), device_id_type=MESH,
        ).start()

    place = lax.broadcasted_iota(jnp.int32, (slots, tiles), 1) * slots + lax.broadcasted_iota(
        jnp.int32, (slots, tiles), 0
    )

    def find(block, found):
        for source in range(sources):
            found = jnp.where(place == pos_ref[source, block], block * sources + source, found)
        return found

    users_v[...] = lax.fori_loop(0, blocks, find, jnp.zeros((slots, tiles), jnp.int32), unroll=8)
    move_users = pltpu.make_async_copy(users_v, users, users_sem)
    move_users.start()

    for copy in send_edges:
        copy.wait()

    def spread(ref, width):
        number = lax.broadcasted_iota(jnp.int32, (fields, width), 0)
        values = jnp.zeros((fields, width), jnp.float32)
        for field in range(fields):
            values = jnp.where(number == field, ref[0, field], values)
        return values

    rates = spread(diffusion_ref, columns)
    gains[...] = spread(coupling_ref, BLOCK)

    def across(value):
        return pltpu.roll(value, 1, 1) + pltpu.roll(value, columns - 1, 1)

    for end, row in ((1, 0), (0, rows - 1)):
        near, far = halo[end, 0:fields], halo[end, fields:2 * fields]
        total = far + line(row) + across(near) - 4.0 * near
        side[end] = near + rates * halo[end, 2 * fields:2 * fields + 1] * total

    row_number = lax.broadcasted_iota(jnp.int32, (rows, columns), 0)

    def substep(value, first, last, rate):
        up = jnp.where(row_number == 0, first, pltpu.roll(value, 1, 0))
        down = jnp.where(row_number == rows - 1, last, pltpu.roll(value, rows - 1, 0))
        total = up + down + across(value) - 4.0 * value
        return value + rate * cover[...] * total

    @pl.loop(0, fields)
    def _(field):
        here = pl.ds(pl.multiple_of(field * rows, rows), rows)
        rate = diffusion_ref[0, field]
        value = whole(cells, here)
        value = substep(value, halo[1, pl.ds(field, 1)], halo[0, pl.ds(field, 1)], rate)
        value = substep(value, side[1, pl.ds(field, 1)], side[0, pl.ds(field, 1)], rate)
        for half in range(halves):
            stepped[half, here] = value[:, half * BLOCK:(half + 1) * BLOCK]

    move_users.wait()
    load_weights.wait()

    @pl.loop(0, tiles // GROUP)
    def _(group):
        froms = [target_tile(me, group * GROUP + turn, tiles) for turn in range(GROUP)]
        for tile in froms:
            arrived = inbox.at[pl.ds(tile * slots, slots)]
            pltpu.make_async_copy(arrived, arrived, box_recv.at[tile]).wait()
        for tile in froms:
            for slot in range(0, slots, 2):
                first = tile * slots + slot
                nothing = jnp.zeros((fields, BLOCK), jnp.bfloat16)
                picked = jnp.concatenate([
                    jnp.concatenate([inbox[first], nothing], axis=1),
                    jnp.concatenate([nothing, inbox[first + 1]], axis=1),
                ], axis=0)
                weight = jnp.concatenate(
                    [weights[users[slot, tile]], weights[users[slot + 1, tile]]], axis=1
                )
                pair = lax.dot_general(
                    picked, weight, (((1,), (1,)), ((), ())), preferred_element_type=jnp.float32
                )
                products[first] = pair[:fields]
                products[first + 1] = pair[fields:]

    pltpu.make_async_copy(outbox, outbox, box_send).wait()


def finish(
    fields, rows, columns, sources,
    products, stepped, cover, gains, pos_ref, new_hbm, flux_hbm, new, flux, new_sem, flux_sem,
):
    halves = columns // BLOCK
    copies = []
    for group in range(rows // GROUP_ROWS):
        for row in range(group * GROUP_ROWS, (group + 1) * GROUP_ROWS):
            lines = pl.ds(row, fields, stride=rows)
            for half in range(halves):
                block = row * halves + half
                total = products[pos_ref[0, block]]
                for source in range(1, sources):
                    total += products[pos_ref[source, block]]
                flux[half, lines] = total
                new[half, lines] = stepped[half, lines] + (
                    gains[...] * cover[row:row + 1, half * BLOCK:(half + 1) * BLOCK] * total
                )
        here = pl.ds(group * GROUP_ROWS, GROUP_ROWS)
        for number, (source, target, sem) in enumerate(((new, new_hbm, new_sem), (flux, flux_hbm, flux_sem))):
            for half in range(halves):
                copy = pltpu.make_async_copy(
                    source.reshape(halves, fields, rows, BLOCK).at[half, :, here],
                    target.at[:, here, pl.ds(half * BLOCK, BLOCK)],
                    sem.at[group, half],
                )
                copy.start()
                copies.append(copy)
    for copy in copies:
        copy.wait()


def per_device(tiles, state, weights, send_slots, recv_pos, diffusion, coupling, sea_mask):
    _, fields, rows, columns = state.shape
    blocks, sources = recv_pos.shape[1:]
    slots = send_slots.shape[3]
    halves = columns // BLOCK
    vmem, smem, hbm = (pl.BlockSpec(memory_space=m) for m in (pltpu.VMEM, pltpu.SMEM, pltpu.HBM))
    edge_rows = 2 * fields + 8
    dma = pltpu.SemaphoreType.DMA
    operands = (
        state.reshape(fields * rows, columns), weights.reshape(blocks * sources, BLOCK, BLOCK),
        send_slots[0, 0].T, recv_pos[0].T, diffusion, coupling, sea_mask,
    )
    between = pl.pallas_call(
        functools.partial(exchange, tiles, slots, fields, rows, columns, blocks, sources),
        out_shape=(
            pltpu.VMEM((tiles * slots, fields, BLOCK), jnp.float32),
            pltpu.VMEM((halves, fields * rows, BLOCK), jnp.float32),
            pltpu.VMEM((rows, columns), jnp.float32),
            pltpu.VMEM((fields, BLOCK), jnp.float32),
            pltpu.SMEM((sources, blocks), jnp.int32),
        ),
        in_specs=[hbm] * 7,
        out_specs=(vmem, vmem, vmem, vmem, smem),
        scratch_shapes=[
            pltpu.SMEM((1, fields), jnp.float32),
            pltpu.SMEM((1, fields), jnp.float32),
            pltpu.VMEM((rows, columns), jnp.int32),
            pltpu.VMEM((halves, fields * rows, BLOCK), jnp.float32),
            pltpu.VMEM((blocks * sources, BLOCK, BLOCK), jnp.bfloat16),
            pltpu.VMEM((blocks, fields, BLOCK), jnp.bfloat16),
            pltpu.SMEM((slots, tiles), jnp.int32),
            pltpu.VMEM((tiles, slots, fields, BLOCK), jnp.bfloat16),
            pltpu.VMEM((tiles * slots, fields, BLOCK), jnp.bfloat16),
            pltpu.VMEM((2, edge_rows, columns), jnp.float32),
            pltpu.VMEM((2, edge_rows, columns), jnp.float32),
            pltpu.VMEM((2, fields, columns), jnp.float32),
            pltpu.VMEM((slots, tiles), jnp.int32),
            pltpu.SMEM((slots, tiles), jnp.int32),
            dma((4,)), dma((halves,)), dma, dma, dma((2,)), dma((2,)), dma, dma, dma, dma((tiles,)),
        ],
        compiler_params=pltpu.CompilerParams(
            collective_id=0, has_side_effects=True, vmem_limit_bytes=32 * 2**20
        ),
    )(*(pltpu.with_memory_space_constraint(value, pltpu.HBM) for value in operands))
    result = jax.ShapeDtypeStruct((fields, rows, columns), jnp.float32)
    groups = rows // GROUP_ROWS
    new, flux = pl.pallas_call(
        functools.partial(finish, fields, rows, columns, sources),
        out_shape=(result, result),
        in_specs=[vmem, vmem, vmem, vmem, smem],
        out_specs=(hbm, hbm),
        scratch_shapes=[
            pltpu.VMEM((halves, fields * rows, BLOCK), jnp.float32),
            pltpu.VMEM((halves, fields * rows, BLOCK), jnp.float32),
            dma((groups, halves)), dma((groups, halves)),
        ],
        compiler_params=pltpu.CompilerParams(vmem_limit_bytes=32 * 2**20),
    )(*between)
    return new[None], flux[None]


def solution(mesh):
    return jax.shard_map(
        functools.partial(per_device, mesh.shape["tile"]),
        mesh=mesh,
        in_specs=(
            P("comp", None, "tile", None),
            P("comp", "tile", None, None, None),
            P("comp", "tile", None, None),
            P("comp", "tile", None),
            P("comp", None),
            P("comp", None),
            P("tile", None),
        ),
        out_specs=(P("comp", None, "tile", None), P("comp", None, "tile", None)),
        check_vma=False,
    )
```

```python
import functools

import jax
import jax.numpy as jnp
from jax import lax
from jax.experimental import pallas as pl
from jax.experimental.pallas import tpu as pltpu
from jax.sharding import PartitionSpec as P

BLOCK = 128
GROUP = 4
GROUP_ROWS = 8
MESH = pl.DeviceIdType.MESH


def target_tile(me, step, tiles):
    if tiles != 64:
        return lax.rem(me + step, tiles)
    x, turn, part = step % 4, step // 4 % 4, step // 16
    y, z_hi, core = (x + turn) % 4, (x // 2 + turn + part) % 2, (part // 2 + x) % 2
    return me ^ (z_hi * 32 + x * 8 + y * 2 + core)


def exchange(
    tiles, slots, fields, rows, columns, blocks, sources,
    state_hbm, weights_hbm, lists_hbm, pos_hbm, diffusion_hbm, coupling_hbm, mask_hbm,
    products, stepped, cover, gains, pos_ref,
    diffusion_ref, coupling_ref, mask_ref, cells, weights, surface, lists, outbox, inbox, edge, halo, side, users_v, users,
    small_sem, state_sem, weights_sem, users_sem, edge_send, edge_recv, list_send, list_recv, box_send, box_recv,
):
    comp, me = lax.axis_index("comp"), lax.axis_index("tile")
    other = 1 - comp
    above, below = (me + tiles - 1) % tiles, (me + 1) % tiles
    halves = columns // BLOCK

    load_state = [
        pltpu.make_async_copy(
            state_hbm.at[:, pl.ds(half * BLOCK, BLOCK)], cells.at[half], state_sem.at[half]
        )
        for half in range(halves)
    ]
    for copy in load_state:
        copy.start()
    load_small = [
        pltpu.make_async_copy(source, target, small_sem.at[number])
        for number, (source, target) in enumerate((
            (pos_hbm, pos_ref), (diffusion_hbm, diffusion_ref),
            (coupling_hbm, coupling_ref), (mask_hbm, mask_ref),
        ))
    ]
    for copy in load_small:
        copy.start()
    load_weights = pltpu.make_async_copy(weights_hbm, weights, weights_sem)
    load_weights.start()

    barrier = pltpu.get_barrier_semaphore()
    for neighbour in (above, below):
        pl.semaphore_signal(barrier, inc=1, device_id=(comp, neighbour), device_id_type=MESH)

    @pl.loop(0, tiles, unroll=tiles)
    def _(step):
        pl.semaphore_signal(
            barrier, inc=1, device_id=(other, target_tile(me, step, tiles)), device_id_type=MESH
        )

    for copy in load_small:
        copy.wait()
    cover[...] = jnp.where(comp == 1, mask_ref[...].astype(jnp.float32), 1.0)
    for copy in load_state:
        copy.wait()

    @pl.loop(0, rows)
    def _(row):
        for half in range(halves):
            picked = cells[half, pl.ds(row, fields, stride=rows)]
            surface[row * halves + half] = picked.astype(jnp.bfloat16)

    def whole(ref, here):
        return jnp.concatenate([ref[half, here] for half in range(halves)], axis=1)

    def line(row):
        return whole(cells, pl.ds(row, fields, stride=rows))

    edge[0, 0:fields] = line(0)
    edge[0, fields:2 * fields] = line(1)
    edge[0, 2 * fields:] = jnp.broadcast_to(cover[0:1], (8, columns))
    edge[1, 0:fields] = line(rows - 1)
    edge[1, fields:2 * fields] = line(rows - 2)
    edge[1, 2 * fields:] = jnp.broadcast_to(cover[rows - 1:rows], (8, columns))

    pl.semaphore_wait(barrier, tiles + 2)

    send_lists = pltpu.make_async_remote_copy(
        src_ref=lists_hbm, dst_ref=lists, send_sem=list_send, recv_sem=list_recv,
        device_id=(other, me), device_id_type=MESH,
    )
    send_lists.start()
    send_edges = [
        pltpu.make_async_remote_copy(
            src_ref=edge.at[end], dst_ref=halo.at[end], send_sem=edge_send.at[end],
            recv_sem=edge_recv.at[end], device_id=(comp, neighbour), device_id_type=MESH,
        )
        for end, neighbour in ((0, above), (1, below))
    ]
    for copy in send_edges:
        copy.start()
    send_lists.wait()

    @pl.loop(0, tiles, unroll=tiles)
    def _(step):
        tile = target_tile(me, step, tiles)
        for slot in range(slots):
            outbox[tile, slot] = surface[lists[slot, tile]]
        pltpu.make_async_remote_copy(
            src_ref=outbox.at[tile], dst_ref=inbox.at[pl.ds(me * slots, slots)],
            send_sem=box_send, recv_sem=box_recv.at[me],
            device_id=(other, tile), device_id_type=MESH,
        ).start()

    place = lax.broadcasted_iota(jnp.int32, (slots, tiles), 1) * slots + lax.broadcasted_iota(
        jnp.int32, (slots, tiles), 0
    )

    def find(block, found):
        for source in range(sources):
            found = jnp.where(place == pos_ref[source, block], block * sources + source, found)
        return found

    users_v[...] = lax.fori_loop(0, blocks, find, jnp.zeros((slots, tiles), jnp.int32), unroll=8)
    move_users = pltpu.make_async_copy(users_v, users, users_sem)
    move_users.start()

    for copy in send_edges:
        copy.wait()

    def spread(ref, width):
        number = lax.broadcasted_iota(jnp.int32, (fields, width), 0)
        values = jnp.zeros((fields, width), jnp.float32)
        for field in range(fields):
            values = jnp.where(number == field, ref[0, field], values)
        return values

    rates = spread(diffusion_ref, columns)
    gains[...] = spread(coupling_ref, BLOCK)

    def across(value):
        return pltpu.roll(value, 1, 1) + pltpu.roll(value, columns - 1, 1)

    for end, row in ((1, 0), (0, rows - 1)):
        near, far = halo[end, 0:fields], halo[end, fields:2 * fields]
        total = far + line(row) + across(near) - 4.0 * near
        side[end] = near + rates * halo[end, 2 * fields:2 * fields + 1] * total

    row_number = lax.broadcasted_iota(jnp.int32, (rows, columns), 0)

    def substep(value, first, last, rate):
        up = jnp.where(row_number == 0, first, pltpu.roll(value, 1, 0))
        down = jnp.where(row_number == rows - 1, last, pltpu.roll(value, rows - 1, 0))
        total = up + down + across(value) - 4.0 * value
        return value + rate * cover[...] * total

    @pl.loop(0, fields)
    def _(field):
        here = pl.ds(pl.multiple_of(field * rows, rows), rows)
        rate = diffusion_ref[0, field]
        value = whole(cells, here)
        value = substep(value, halo[1, pl.ds(field, 1)], halo[0, pl.ds(field, 1)], rate)
        value = substep(value, side[1, pl.ds(field, 1)], side[0, pl.ds(field, 1)], rate)
        for half in range(halves):
            stepped[half, here] = value[:, half * BLOCK:(half + 1) * BLOCK]

    move_users.wait()
    load_weights.wait()

    @pl.loop(0, tiles // GROUP)
    def _(group):
        froms = [target_tile(me, group * GROUP + turn, tiles) for turn in range(GROUP)]
        for tile in froms:
            arrived = inbox.at[pl.ds(tile * slots, slots)]
            pltpu.make_async_copy(arrived, arrived, box_recv.at[tile]).wait()
        for tile in froms:
            for slot in range(0, slots, 2):
                first = tile * slots + slot
                nothing = jnp.zeros((fields, BLOCK), jnp.bfloat16)
                picked = jnp.concatenate([
                    jnp.concatenate([inbox[first], nothing], axis=1),
                    jnp.concatenate([nothing, inbox[first + 1]], axis=1),
                ], axis=0)
                weight = jnp.concatenate(
                    [weights[users[slot, tile]], weights[users[slot + 1, tile]]], axis=1
                )
                pair = lax.dot_general(
                    picked, weight, (((1,), (1,)), ((), ())), preferred_element_type=jnp.float32
                )
                products[first] = pair[:fields]
                products[first + 1] = pair[fields:]

    pltpu.make_async_copy(outbox, outbox, box_send).wait()


def finish(
    fields, rows, columns, sources,
    products, stepped, cover, gains, pos_ref, new_hbm, flux_hbm, new, flux, new_sem, flux_sem,
):
    halves = columns // BLOCK
    copies = []
    for group in range(rows // GROUP_ROWS):
        for row in range(group * GROUP_ROWS, (group + 1) * GROUP_ROWS):
            lines = pl.ds(row, fields, stride=rows)
            for half in range(halves):
                block = row * halves + half
                total = products[pos_ref[0, block]]
                for source in range(1, sources):
                    total += products[pos_ref[source, block]]
                flux[half, lines] = total
                new[half, lines] = stepped[half, lines] + (
                    gains[...] * cover[row:row + 1, half * BLOCK:(half + 1) * BLOCK] * total
                )
        here = pl.ds(group * GROUP_ROWS, GROUP_ROWS)
        for number, (source, target, sem) in enumerate(((new, new_hbm, new_sem), (flux, flux_hbm, flux_sem))):
            for half in range(halves):
                copy = pltpu.make_async_copy(
                    source.reshape(halves, fields, rows, BLOCK).at[half, :, here],
                    target.at[:, here, pl.ds(half * BLOCK, BLOCK)],
                    sem.at[group, half],
                )
                copy.start()
                copies.append(copy)
    for copy in copies:
        copy.wait()


def per_device(tiles, state, weights, send_slots, recv_pos, diffusion, coupling, sea_mask):
    _, fields, rows, columns = state.shape
    blocks, sources = recv_pos.shape[1:]
    slots = send_slots.shape[3]
    halves = columns // BLOCK
    vmem, smem, hbm = (pl.BlockSpec(memory_space=m) for m in (pltpu.VMEM, pltpu.SMEM, pltpu.HBM))
    edge_rows = 2 * fields + 8
    dma = pltpu.SemaphoreType.DMA
    operands = (
        state.reshape(fields * rows, columns), weights.reshape(blocks * sources, BLOCK, BLOCK),
        send_slots[0, 0].T, recv_pos[0].T, diffusion, coupling, sea_mask,
    )
    between = pl.pallas_call(
        functools.partial(exchange, tiles, slots, fields, rows, columns, blocks, sources),
        out_shape=(
            pltpu.VMEM((tiles * slots, fields, BLOCK), jnp.float32),
            pltpu.VMEM((halves, fields * rows, BLOCK), jnp.float32),
            pltpu.VMEM((rows, columns), jnp.float32),
            pltpu.VMEM((fields, BLOCK), jnp.float32),
            pltpu.SMEM((sources, blocks), jnp.int32),
        ),
        in_specs=[hbm] * 7,
        out_specs=(vmem, vmem, vmem, vmem, smem),
        scratch_shapes=[
            pltpu.SMEM((1, fields), jnp.float32),
            pltpu.SMEM((1, fields), jnp.float32),
            pltpu.VMEM((rows, columns), jnp.int32),
            pltpu.VMEM((halves, fields * rows, BLOCK), jnp.float32),
            pltpu.VMEM((blocks * sources, BLOCK, BLOCK), jnp.bfloat16),
            pltpu.VMEM((blocks, fields, BLOCK), jnp.bfloat16),
            pltpu.SMEM((slots, tiles), jnp.int32),
            pltpu.VMEM((tiles, slots, fields, BLOCK), jnp.bfloat16),
            pltpu.VMEM((tiles * slots, fields, BLOCK), jnp.bfloat16),
            pltpu.VMEM((2, edge_rows, columns), jnp.float32),
            pltpu.VMEM((2, edge_rows, columns), jnp.float32),
            pltpu.VMEM((2, fields, columns), jnp.float32),
            pltpu.VMEM((slots, tiles), jnp.int32),
            pltpu.SMEM((slots, tiles), jnp.int32),
            dma((4,)), dma((halves,)), dma, dma, dma((2,)), dma((2,)), dma, dma, dma, dma((tiles,)),
        ],
        compiler_params=pltpu.CompilerParams(
            collective_id=0, has_side_effects=True, vmem_limit_bytes=32 * 2**20
        ),
    )(*(pltpu.with_memory_space_constraint(value, pltpu.HBM) for value in operands))
    result = jax.ShapeDtypeStruct((fields, rows, columns), jnp.float32)
    groups = rows // GROUP_ROWS
    new, flux = pl.pallas_call(
        functools.partial(finish, fields, rows, columns, sources),
        out_shape=(result, result),
        in_specs=[vmem, vmem, vmem, vmem, smem],
        out_specs=(hbm, hbm),
        scratch_shapes=[
            pltpu.VMEM((halves, fields * rows, BLOCK), jnp.float32),
            pltpu.VMEM((halves, fields * rows, BLOCK), jnp.float32),
            dma((groups, halves)), dma((groups, halves)),
        ],
        compiler_params=pltpu.CompilerParams(vmem_limit_bytes=32 * 2**20),
    )(*between)
    return new[None], flux[None]


def solution(mesh):
    return jax.shard_map(
        functools.partial(per_device, mesh.shape["tile"]),
        mesh=mesh,
        in_specs=(
            P("comp", None, "tile", None),
            P("comp", "tile", None, None, None),
            P("comp", "tile", None, None),
            P("comp", "tile", None),
            P("comp", None),
            P("comp", None),
            P("tile", None),
        ),
        out_specs=(P("comp", None, "tile", None), P("comp", None, "tile", None)),
        check_vma=False,
    )
```

```python
import functools

import jax
import jax.numpy as jnp
from jax import lax
from jax.experimental import pallas as pl
from jax.experimental.pallas import tpu as pltpu
from jax.sharding import PartitionSpec as P

BLOCK = 128
GROUP = 4
GROUP_ROWS = 8
MESH = pl.DeviceIdType.MESH


def target_tile(me, step, tiles):
    if tiles != 64:
        return lax.rem(me + step, tiles)
    x, turn, part = step % 4, step // 4 % 4, step // 16
    y, z_hi, core = (x + turn) % 4, (x // 2 + turn + part) % 2, (part // 2 + x) % 2
    return me ^ (z_hi * 32 + x * 8 + y * 2 + core)


def exchange(
    tiles, slots, fields, rows, columns, blocks, sources,
    state_hbm, weights_hbm, lists_hbm, pos_hbm, diffusion_hbm, coupling_hbm, mask_hbm,
    products, stepped, cover, coupling_ref, pos_ref,
    diffusion_ref, mask_ref, cells, weights, surface, lists, outbox, inbox, edge, halo, side, users_v, users,
    small_sem, state_sem, weights_sem, users_sem, edge_send, edge_recv, list_send, list_recv, box_send, box_recv,
):
    comp, me = lax.axis_index("comp"), lax.axis_index("tile")
    other = 1 - comp
    above, below = (me + tiles - 1) % tiles, (me + 1) % tiles
    halves = columns // BLOCK

    load_state = [
        pltpu.make_async_copy(
            state_hbm.at[:, pl.ds(half * BLOCK, BLOCK)], cells.at[half], state_sem.at[half]
        )
        for half in range(halves)
    ]
    for copy in load_state:
        copy.start()
    load_small = [
        pltpu.make_async_copy(source, target, small_sem.at[number])
        for number, (source, target) in enumerate((
            (pos_hbm, pos_ref), (diffusion_hbm, diffusion_ref),
            (coupling_hbm, coupling_ref), (mask_hbm, mask_ref),
        ))
    ]
    for copy in load_small:
        copy.start()
    load_weights = pltpu.make_async_copy(weights_hbm, weights, weights_sem)
    load_weights.start()

    barrier = pltpu.get_barrier_semaphore()
    for neighbour in (above, below):
        pl.semaphore_signal(barrier, inc=1, device_id=(comp, neighbour), device_id_type=MESH)

    @pl.loop(0, tiles, unroll=tiles)
    def _(step):
        pl.semaphore_signal(
            barrier, inc=1, device_id=(other, target_tile(me, step, tiles)), device_id_type=MESH
        )

    for copy in load_small:
        copy.wait()
    cover[...] = jnp.where(comp == 1, mask_ref[...].astype(jnp.float32), 1.0)
    for copy in load_state:
        copy.wait()

    @pl.loop(0, rows)
    def _(row):
        for half in range(halves):
            picked = cells[half, pl.ds(row, fields, stride=rows)]
            surface[row * halves + half] = picked.astype(jnp.bfloat16)

    def whole(ref, here):
        return jnp.concatenate([ref[half, here] for half in range(halves)], axis=1)

    def line(row):
        return whole(cells, pl.ds(row, fields, stride=rows))

    edge[0, 0:fields] = line(0)
    edge[0, fields:2 * fields] = line(1)
    edge[0, 2 * fields:] = jnp.broadcast_to(cover[0:1], (8, columns))
    edge[1, 0:fields] = line(rows - 1)
    edge[1, fields:2 * fields] = line(rows - 2)
    edge[1, 2 * fields:] = jnp.broadcast_to(cover[rows - 1:rows], (8, columns))

    pl.semaphore_wait(barrier, tiles + 2)

    send_lists = pltpu.make_async_remote_copy(
        src_ref=lists_hbm, dst_ref=lists, send_sem=list_send, recv_sem=list_recv,
        device_id=(other, me), device_id_type=MESH,
    )
    send_lists.start()
    send_edges = [
        pltpu.make_async_remote_copy(
            src_ref=edge.at[end], dst_ref=halo.at[end], send_sem=edge_send.at[end],
            recv_sem=edge_recv.at[end], device_id=(comp, neighbour), device_id_type=MESH,
        )
        for end, neighbour in ((0, above), (1, below))
    ]
    for copy in send_edges:
        copy.start()
    send_lists.wait()

    @pl.loop(0, tiles, unroll=tiles)
    def _(step):
        tile = target_tile(me, step, tiles)
        for slot in range(slots):
            outbox[tile, slot] = surface[lists[slot, tile]]
        pltpu.make_async_remote_copy(
            src_ref=outbox.at[tile], dst_ref=inbox.at[pl.ds(me * slots, slots)],
            send_sem=box_send, recv_sem=box_recv.at[me],
            device_id=(other, tile), device_id_type=MESH,
        ).start()

    place = lax.broadcasted_iota(jnp.int32, (slots, tiles), 1) * slots + lax.broadcasted_iota(
        jnp.int32, (slots, tiles), 0
    )

    def find(block, found):
        for source in range(sources):
            found = jnp.where(place == pos_ref[source, block], block * sources + source, found)
        return found

    users_v[...] = lax.fori_loop(0, blocks, find, jnp.zeros((slots, tiles), jnp.int32), unroll=8)
    move_users = pltpu.make_async_copy(users_v, users, users_sem)
    move_users.start()

    for copy in send_edges:
        copy.wait()

    number = lax.broadcasted_iota(jnp.int32, (fields, columns), 0)
    rates = jnp.zeros((fields, columns), jnp.float32)
    for field in range(fields):
        rates = jnp.where(number == field, diffusion_ref[0, field], rates)

    def across(value):
        return pltpu.roll(value, 1, 1) + pltpu.roll(value, columns - 1, 1)

    for end, row in ((1, 0), (0, rows - 1)):
        near, far = halo[end, 0:fields], halo[end, fields:2 * fields]
        total = far + line(row) + across(near) - 4.0 * near
        side[end] = near + rates * halo[end, 2 * fields:2 * fields + 1] * total

    row_number = lax.broadcasted_iota(jnp.int32, (rows, columns), 0)

    def substep(value, first, last, rate):
        up = jnp.where(row_number == 0, first, pltpu.roll(value, 1, 0))
        down = jnp.where(row_number == rows - 1, last, pltpu.roll(value, rows - 1, 0))
        total = up + down + across(value) - 4.0 * value
        return value + rate * cover[...] * total

    @pl.loop(0, fields)
    def _(field):
        here = pl.ds(pl.multiple_of(field * rows, rows), rows)
        rate = diffusion_ref[0, field]
        value = whole(cells, here)
        value = substep(value, halo[1, pl.ds(field, 1)], halo[0, pl.ds(field, 1)], rate)
        value = substep(value, side[1, pl.ds(field, 1)], side[0, pl.ds(field, 1)], rate)
        for half in range(halves):
            stepped[half, here] = value[:, half * BLOCK:(half + 1) * BLOCK]

    move_users.wait()
    load_weights.wait()

    @pl.loop(0, tiles // GROUP)
    def _(group):
        froms = [target_tile(me, group * GROUP + turn, tiles) for turn in range(GROUP)]
        for tile in froms:
            arrived = inbox.at[pl.ds(tile * slots, slots)]
            pltpu.make_async_copy(arrived, arrived, box_recv.at[tile]).wait()
        for tile in froms:
            for slot in range(0, slots, 2):
                first = tile * slots + slot
                nothing = jnp.zeros((fields, BLOCK), jnp.bfloat16)
                picked = jnp.concatenate([
                    jnp.concatenate([inbox[first], nothing], axis=1),
                    jnp.concatenate([nothing, inbox[first + 1]], axis=1),
                ], axis=0)
                weight = jnp.concatenate(
                    [weights[users[slot, tile]], weights[users[slot + 1, tile]]], axis=1
                )
                pair = lax.dot_general(
                    picked, weight, (((1,), (1,)), ((), ())), preferred_element_type=jnp.float32
                )
                products[first] = pair[:fields]
                products[first + 1] = pair[fields:]

    pltpu.make_async_copy(outbox, outbox, box_send).wait()


def finish(
    fields, rows, columns, sources,
    products, stepped, cover, coupling_ref, pos_ref, new_hbm, flux_hbm, new, flux, new_sem, flux_sem,
):
    halves = columns // BLOCK
    copies = []
    for group in range(rows // GROUP_ROWS):
        for half in range(halves):
            totals = []
            for row in range(group * GROUP_ROWS, (group + 1) * GROUP_ROWS):
                block = row * halves + half
                total = products[pos_ref[0, block]]
                for source in range(1, sources):
                    total += products[pos_ref[source, block]]
                totals.append(total)
            turned = jnp.swapaxes(jnp.stack(totals), 0, 1)
            for field in range(fields):
                flux[half, pl.ds(field * rows + group * GROUP_ROWS, GROUP_ROWS)] = turned[field]
        shares = cover[group * GROUP_ROWS:(group + 1) * GROUP_ROWS]
        for field in range(fields):
            lines = pl.ds(field * rows + group * GROUP_ROWS, GROUP_ROWS)
            for half in range(halves):
                share = coupling_ref[0, field] * shares[:, half * BLOCK:(half + 1) * BLOCK]
                new[half, lines] = stepped[half, lines] + share * flux[half, lines]
        here = pl.ds(group * GROUP_ROWS, GROUP_ROWS)
        for number, (source, target, sem) in enumerate(((new, new_hbm, new_sem), (flux, flux_hbm, flux_sem))):
            for half in range(halves):
                copy = pltpu.make_async_copy(
                    source.reshape(halves, fields, rows, BLOCK).at[half, :, here],
                    target.at[:, here, pl.ds(half * BLOCK, BLOCK)],
                    sem.at[group, half],
                )
                copy.start()
                copies.append(copy)
    for copy in copies:
        copy.wait()


def per_device(tiles, state, weights, send_slots, recv_pos, diffusion, coupling, sea_mask):
    _, fields, rows, columns = state.shape
    blocks, sources = recv_pos.shape[1:]
    slots = send_slots.shape[3]
    halves = columns // BLOCK
    vmem, smem, hbm = (pl.BlockSpec(memory_space=m) for m in (pltpu.VMEM, pltpu.SMEM, pltpu.HBM))
    edge_rows = 2 * fields + 8
    dma = pltpu.SemaphoreType.DMA
    operands = (
        state.reshape(fields * rows, columns), weights.reshape(blocks * sources, BLOCK, BLOCK),
        send_slots[0, 0].T, recv_pos[0].T, diffusion, coupling, sea_mask,
    )
    between = pl.pallas_call(
        functools.partial(exchange, tiles, slots, fields, rows, columns, blocks, sources),
        out_shape=(
            pltpu.VMEM((tiles * slots, fields, BLOCK), jnp.float32),
            pltpu.VMEM((halves, fields * rows, BLOCK), jnp.float32),
            pltpu.VMEM((rows, columns), jnp.float32),
            pltpu.SMEM((1, fields), jnp.float32),
            pltpu.SMEM((sources, blocks), jnp.int32),
        ),
        in_specs=[hbm] * 7,
        out_specs=(vmem, vmem, vmem, smem, smem),
        scratch_shapes=[
            pltpu.SMEM((1, fields), jnp.float32),
            pltpu.VMEM((rows, columns), jnp.int32),
            pltpu.VMEM((halves, fields * rows, BLOCK), jnp.float32),
            pltpu.VMEM((blocks * sources, BLOCK, BLOCK), jnp.bfloat16),
            pltpu.VMEM((blocks, fields, BLOCK), jnp.bfloat16),
            pltpu.SMEM((slots, tiles), jnp.int32),
            pltpu.VMEM((tiles, slots, fields, BLOCK), jnp.bfloat16),
            pltpu.VMEM((tiles * slots, fields, BLOCK), jnp.bfloat16),
            pltpu.VMEM((2, edge_rows, columns), jnp.float32),
            pltpu.VMEM((2, edge_rows, columns), jnp.float32),
            pltpu.VMEM((2, fields, columns), jnp.float32),
            pltpu.VMEM((slots, tiles), jnp.int32),
            pltpu.SMEM((slots, tiles), jnp.int32),
            dma((4,)), dma((halves,)), dma, dma, dma((2,)), dma((2,)), dma, dma, dma, dma((tiles,)),
        ],
        compiler_params=pltpu.CompilerParams(
            collective_id=0, has_side_effects=True, vmem_limit_bytes=32 * 2**20
        ),
    )(*(pltpu.with_memory_space_constraint(value, pltpu.HBM) for value in operands))
    result = jax.ShapeDtypeStruct((fields, rows, columns), jnp.float32)
    groups = rows // GROUP_ROWS
    new, flux = pl.pallas_call(
        functools.partial(finish, fields, rows, columns, sources),
        out_shape=(result, result),
        in_specs=[vmem, vmem, vmem, smem, smem],
        out_specs=(hbm, hbm),
        scratch_shapes=[
            pltpu.VMEM((halves, fields * rows, BLOCK), jnp.float32),
            pltpu.VMEM((halves, fields * rows, BLOCK), jnp.float32),
            dma((groups, halves)), dma((groups, halves)),
        ],
        compiler_params=pltpu.CompilerParams(vmem_limit_bytes=32 * 2**20),
    )(*between)
    return new[None], flux[None]


def solution(mesh):
    return jax.shard_map(
        functools.partial(per_device, mesh.shape["tile"]),
        mesh=mesh,
        in_specs=(
            P("comp", None, "tile", None),
            P("comp", "tile", None, None, None),
            P("comp", "tile", None, None),
            P("comp", "tile", None),
            P("comp", None),
            P("comp", None),
            P("tile", None),
        ),
        out_specs=(P("comp", None, "tile", None), P("comp", None, "tile", None)),
        check_vma=False,
    )
```

```python
import functools

import jax
import jax.numpy as jnp
from jax import lax
from jax.experimental import pallas as pl
from jax.experimental.pallas import tpu as pltpu
from jax.sharding import PartitionSpec as P

BLOCK = 128
GROUP = 4
GROUP_ROWS = 8
MESH = pl.DeviceIdType.MESH


def target_tile(me, step, tiles):
    if tiles != 64:
        return lax.rem(me + step, tiles)
    x, turn, part = step % 4, step // 4 % 4, step // 16
    y, z_hi, core = (x + turn) % 4, (x + turn + part) % 2, (part // 2 + x // 2) % 2
    return me ^ (z_hi * 32 + x * 8 + y * 2 + core)


def exchange(
    tiles, slots, fields, rows, columns, blocks, sources,
    state_hbm, weights_hbm, lists_hbm, pos_hbm, diffusion_hbm, coupling_hbm, mask_hbm,
    products, stepped, cover, coupling_ref, pos_ref,
    diffusion_ref, mask_ref, cells, weights, surface, lists, outbox, inbox, edge, halo, side, users_v, users,
    small_sem, state_sem, weights_sem, users_sem, edge_send, edge_recv, list_send, list_recv, box_send, box_recv,
):
    comp, me = lax.axis_index("comp"), lax.axis_index("tile")
    other = 1 - comp
    above, below = (me + tiles - 1) % tiles, (me + 1) % tiles
    halves = columns // BLOCK

    load_state = [
        pltpu.make_async_copy(
            state_hbm.at[:, pl.ds(half * BLOCK, BLOCK)], cells.at[half], state_sem.at[half]
        )
        for half in range(halves)
    ]
    for copy in load_state:
        copy.start()
    load_small = [
        pltpu.make_async_copy(source, target, small_sem.at[number])
        for number, (source, target) in enumerate((
            (pos_hbm, pos_ref), (diffusion_hbm, diffusion_ref),
            (coupling_hbm, coupling_ref), (mask_hbm, mask_ref),
        ))
    ]
    for copy in load_small:
        copy.start()
    load_weights = pltpu.make_async_copy(weights_hbm, weights, weights_sem)
    load_weights.start()

    barrier = pltpu.get_barrier_semaphore()
    for neighbour in (above, below):
        pl.semaphore_signal(barrier, inc=1, device_id=(comp, neighbour), device_id_type=MESH)

    @pl.loop(0, tiles, unroll=tiles)
    def _(step):
        pl.semaphore_signal(
            barrier, inc=1, device_id=(other, target_tile(me, step, tiles)), device_id_type=MESH
        )

    for copy in load_small:
        copy.wait()
    cover[...] = jnp.where(comp == 1, mask_ref[...].astype(jnp.float32), 1.0)
    for copy in load_state:
        copy.wait()

    @pl.loop(0, rows)
    def _(row):
        for half in range(halves):
            picked = cells[half, pl.ds(row, fields, stride=rows)]
            surface[row * halves + half] = picked.astype(jnp.bfloat16)

    def whole(ref, here):
        return jnp.concatenate([ref[half, here] for half in range(halves)], axis=1)

    def line(row):
        return whole(cells, pl.ds(row, fields, stride=rows))

    edge[0, 0:fields] = line(0)
    edge[0, fields:2 * fields] = line(1)
    edge[0, 2 * fields:] = jnp.broadcast_to(cover[0:1], (8, columns))
    edge[1, 0:fields] = line(rows - 1)
    edge[1, fields:2 * fields] = line(rows - 2)
    edge[1, 2 * fields:] = jnp.broadcast_to(cover[rows - 1:rows], (8, columns))

    pl.semaphore_wait(barrier, tiles + 2)

    send_lists = pltpu.make_async_remote_copy(
        src_ref=lists_hbm, dst_ref=lists, send_sem=list_send, recv_sem=list_recv,
        device_id=(other, me), device_id_type=MESH,
    )
    send_lists.start()
    send_edges = [
        pltpu.make_async_remote_copy(
            src_ref=edge.at[end], dst_ref=halo.at[end], send_sem=edge_send.at[end],
            recv_sem=edge_recv.at[end], device_id=(comp, neighbour), device_id_type=MESH,
        )
        for end, neighbour in ((0, above), (1, below))
    ]
    for copy in send_edges:
        copy.start()
    send_lists.wait()

    @pl.loop(0, tiles, unroll=tiles)
    def _(step):
        tile = target_tile(me, step, tiles)
        for slot in range(slots):
            outbox[tile, slot] = surface[lists[slot, tile]]
        pltpu.make_async_remote_copy(
            src_ref=outbox.at[tile], dst_ref=inbox.at[pl.ds(me * slots, slots)],
            send_sem=box_send, recv_sem=box_recv.at[me],
            device_id=(other, tile), device_id_type=MESH,
        ).start()

    place = lax.broadcasted_iota(jnp.int32, (slots, tiles), 1) * slots + lax.broadcasted_iota(
        jnp.int32, (slots, tiles), 0
    )

    def find(block, found):
        for source in range(sources):
            found = jnp.where(place == pos_ref[source, block], block * sources + source, found)
        return found

    users_v[...] = lax.fori_loop(0, blocks, find, jnp.zeros((slots, tiles), jnp.int32), unroll=8)
    move_users = pltpu.make_async_copy(users_v, users, users_sem)
    move_users.start()

    for copy in send_edges:
        copy.wait()

    number = lax.broadcasted_iota(jnp.int32, (fields, columns), 0)
    rates = jnp.zeros((fields, columns), jnp.float32)
    for field in range(fields):
        rates = jnp.where(number == field, diffusion_ref[0, field], rates)

    def across(value):
        return pltpu.roll(value, 1, 1) + pltpu.roll(value, columns - 1, 1)

    for end, row in ((1, 0), (0, rows - 1)):
        near, far = halo[end, 0:fields], halo[end, fields:2 * fields]
        total = far + line(row) + across(near) - 4.0 * near
        side[end] = near + rates * halo[end, 2 * fields:2 * fields + 1] * total

    row_number = lax.broadcasted_iota(jnp.int32, (rows, columns), 0)

    def substep(value, first, last, rate):
        up = jnp.where(row_number == 0, first, pltpu.roll(value, 1, 0))
        down = jnp.where(row_number == rows - 1, last, pltpu.roll(value, rows - 1, 0))
        total = up + down + across(value) - 4.0 * value
        return value + rate * cover[...] * total

    @pl.loop(0, fields)
    def _(field):
        here = pl.ds(pl.multiple_of(field * rows, rows), rows)
        rate = diffusion_ref[0, field]
        value = whole(cells, here)
        value = substep(value, halo[1, pl.ds(field, 1)], halo[0, pl.ds(field, 1)], rate)
        value = substep(value, side[1, pl.ds(field, 1)], side[0, pl.ds(field, 1)], rate)
        for half in range(halves):
            stepped[half, here] = value[:, half * BLOCK:(half + 1) * BLOCK]

    move_users.wait()
    load_weights.wait()

    @pl.loop(0, tiles // GROUP)
    def _(group):
        froms = [target_tile(me, group * GROUP + turn, tiles) for turn in range(GROUP)]
        for tile in froms:
            arrived = inbox.at[pl.ds(tile * slots, slots)]
            pltpu.make_async_copy(arrived, arrived, box_recv.at[tile]).wait()
        for tile in froms:
            for slot in range(0, slots, 2):
                first = tile * slots + slot
                nothing = jnp.zeros((fields, BLOCK), jnp.bfloat16)
                picked = jnp.concatenate([
                    jnp.concatenate([inbox[first], nothing], axis=1),
                    jnp.concatenate([nothing, inbox[first + 1]], axis=1),
                ], axis=0)
                weight = jnp.concatenate(
                    [weights[users[slot, tile]], weights[users[slot + 1, tile]]], axis=1
                )
                pair = lax.dot_general(
                    picked, weight, (((1,), (1,)), ((), ())), preferred_element_type=jnp.float32
                )
                products[first] = pair[:fields]
                products[first + 1] = pair[fields:]

    pltpu.make_async_copy(outbox, outbox, box_send).wait()


def finish(
    fields, rows, columns, sources,
    products, stepped, cover, coupling_ref, pos_ref, new_hbm, flux_hbm, new, flux, new_sem, flux_sem,
):
    halves = columns // BLOCK
    copies = []
    for group in range(rows // GROUP_ROWS):
        for half in range(halves):
            totals = []
            for row in range(group * GROUP_ROWS, (group + 1) * GROUP_ROWS):
                block = row * halves + half
                total = products[pos_ref[0, block]]
                for source in range(1, sources):
                    total += products[pos_ref[source, block]]
                totals.append(total)
            turned = jnp.swapaxes(jnp.stack(totals), 0, 1)
            for field in range(fields):
                flux[half, pl.ds(field * rows + group * GROUP_ROWS, GROUP_ROWS)] = turned[field]
        shares = cover[group * GROUP_ROWS:(group + 1) * GROUP_ROWS]
        for field in range(fields):
            lines = pl.ds(field * rows + group * GROUP_ROWS, GROUP_ROWS)
            for half in range(halves):
                share = coupling_ref[0, field] * shares[:, half * BLOCK:(half + 1) * BLOCK]
                new[half, lines] = stepped[half, lines] + share * flux[half, lines]
        here = pl.ds(group * GROUP_ROWS, GROUP_ROWS)
        for number, (source, target, sem) in enumerate(((new, new_hbm, new_sem), (flux, flux_hbm, flux_sem))):
            for half in range(halves):
                copy = pltpu.make_async_copy(
                    source.reshape(halves, fields, rows, BLOCK).at[half, :, here],
                    target.at[:, here, pl.ds(half * BLOCK, BLOCK)],
                    sem.at[group, half],
                )
                copy.start()
                copies.append(copy)
    for copy in copies:
        copy.wait()


def per_device(tiles, state, weights, send_slots, recv_pos, diffusion, coupling, sea_mask):
    _, fields, rows, columns = state.shape
    blocks, sources = recv_pos.shape[1:]
    slots = send_slots.shape[3]
    halves = columns // BLOCK
    vmem, smem, hbm = (pl.BlockSpec(memory_space=m) for m in (pltpu.VMEM, pltpu.SMEM, pltpu.HBM))
    edge_rows = 2 * fields + 8
    dma = pltpu.SemaphoreType.DMA
    operands = (
        state.reshape(fields * rows, columns), weights.reshape(blocks * sources, BLOCK, BLOCK),
        send_slots[0, 0].T, recv_pos[0].T, diffusion, coupling, sea_mask,
    )
    between = pl.pallas_call(
        functools.partial(exchange, tiles, slots, fields, rows, columns, blocks, sources),
        out_shape=(
            pltpu.VMEM((tiles * slots, fields, BLOCK), jnp.float32),
            pltpu.VMEM((halves, fields * rows, BLOCK), jnp.float32),
            pltpu.VMEM((rows, columns), jnp.float32),
            pltpu.SMEM((1, fields), jnp.float32),
            pltpu.SMEM((sources, blocks), jnp.int32),
        ),
        in_specs=[hbm] * 7,
        out_specs=(vmem, vmem, vmem, smem, smem),
        scratch_shapes=[
            pltpu.SMEM((1, fields), jnp.float32),
            pltpu.VMEM((rows, columns), jnp.int32),
            pltpu.VMEM((halves, fields * rows, BLOCK), jnp.float32),
            pltpu.VMEM((blocks * sources, BLOCK, BLOCK), jnp.bfloat16),
            pltpu.VMEM((blocks, fields, BLOCK), jnp.bfloat16),
            pltpu.SMEM((slots, tiles), jnp.int32),
            pltpu.VMEM((tiles, slots, fields, BLOCK), jnp.bfloat16),
            pltpu.VMEM((tiles * slots, fields, BLOCK), jnp.bfloat16),
            pltpu.VMEM((2, edge_rows, columns), jnp.float32),
            pltpu.VMEM((2, edge_rows, columns), jnp.float32),
            pltpu.VMEM((2, fields, columns), jnp.float32),
            pltpu.VMEM((slots, tiles), jnp.int32),
            pltpu.SMEM((slots, tiles), jnp.int32),
            dma((4,)), dma((halves,)), dma, dma, dma((2,)), dma((2,)), dma, dma, dma, dma((tiles,)),
        ],
        compiler_params=pltpu.CompilerParams(
            collective_id=0, has_side_effects=True, vmem_limit_bytes=32 * 2**20
        ),
    )(*(pltpu.with_memory_space_constraint(value, pltpu.HBM) for value in operands))
    result = jax.ShapeDtypeStruct((fields, rows, columns), jnp.float32)
    groups = rows // GROUP_ROWS
    new, flux = pl.pallas_call(
        functools.partial(finish, fields, rows, columns, sources),
        out_shape=(result, result),
        in_specs=[vmem, vmem, vmem, smem, smem],
        out_specs=(hbm, hbm),
        scratch_shapes=[
            pltpu.VMEM((halves, fields * rows, BLOCK), jnp.float32),
            pltpu.VMEM((halves, fields * rows, BLOCK), jnp.float32),
            dma((groups, halves)), dma((groups, halves)),
        ],
        compiler_params=pltpu.CompilerParams(vmem_limit_bytes=32 * 2**20),
    )(*between)
    return new[None], flux[None]


def solution(mesh):
    return jax.shard_map(
        functools.partial(per_device, mesh.shape["tile"]),
        mesh=mesh,
        in_specs=(
            P("comp", None, "tile", None),
            P("comp", "tile", None, None, None),
            P("comp", "tile", None, None),
            P("comp", "tile", None),
            P("comp", None),
            P("comp", None),
            P("tile", None),
        ),
        out_specs=(P("comp", None, "tile", None), P("comp", None, "tile", None)),
        check_vma=False,
    )
```

```python
import functools

import jax
import jax.numpy as jnp
from jax import lax
from jax.experimental import pallas as pl
from jax.experimental.pallas import tpu as pltpu
from jax.sharding import PartitionSpec as P

BLOCK = 128
GROUP = 4
GROUP_ROWS = 8
MESH = pl.DeviceIdType.MESH


def target_tile_offset(step):
    x, turn, part = step % 4, (step // 4 + 1) % 4, step // 16
    y, z_hi, core = (x + turn) % 4, (x + turn + part) % 2, (part // 2 + x // 2) % 2
    return z_hi * 32 + x * 8 + y * 2 + core


def target_tile(me, step, tiles):
    if tiles != 64:
        return lax.rem(me + step, tiles)
    return me ^ target_tile_offset(step)


def hops(tiles, step):
    offset = target_tile_offset(step) if tiles == 64 else 0
    return sum((0, 1, 2, 1)[offset // low % 4] for low in (2, 8))


def exchange(
    tiles, slots, fields, rows, columns, blocks, sources,
    state_hbm, weights_hbm, lists_hbm, pos_hbm, diffusion_hbm, coupling_hbm, mask_hbm,
    products, stepped, cover, coupling_ref, pos_ref,
    diffusion_ref, mask_ref, cells, weights, surface, lists, outbox, inbox, edge, halo, side, users_v, users,
    small_sem, state_sem, weights_sem, users_sem, edge_send, edge_recv, list_send, list_recv, box_send, box_recv,
):
    comp, me = lax.axis_index("comp"), lax.axis_index("tile")
    other = 1 - comp
    above, below = (me + tiles - 1) % tiles, (me + 1) % tiles
    halves = columns // BLOCK

    load_state = [
        pltpu.make_async_copy(
            state_hbm.at[:, pl.ds(half * BLOCK, BLOCK)], cells.at[half], state_sem.at[half]
        )
        for half in range(halves)
    ]
    for copy in load_state:
        copy.start()
    load_small = [
        pltpu.make_async_copy(source, target, small_sem.at[number])
        for number, (source, target) in enumerate((
            (pos_hbm, pos_ref), (diffusion_hbm, diffusion_ref),
            (coupling_hbm, coupling_ref), (mask_hbm, mask_ref),
        ))
    ]
    for copy in load_small:
        copy.start()
    load_weights = pltpu.make_async_copy(weights_hbm, weights, weights_sem)
    load_weights.start()

    barrier = pltpu.get_barrier_semaphore()
    for neighbour in (above, below):
        pl.semaphore_signal(barrier, inc=1, device_id=(comp, neighbour), device_id_type=MESH)

    for step in sorted(range(tiles), key=functools.partial(hops, tiles), reverse=True):
        pl.semaphore_signal(
            barrier, inc=1, device_id=(other, target_tile(me, step, tiles)), device_id_type=MESH
        )

    for copy in load_small:
        copy.wait()
    cover[...] = jnp.where(comp == 1, mask_ref[...].astype(jnp.float32), 1.0)
    for copy in load_state:
        copy.wait()

    @pl.loop(0, rows)
    def _(row):
        for half in range(halves):
            picked = cells[half, pl.ds(row, fields, stride=rows)]
            surface[row * halves + half] = picked.astype(jnp.bfloat16)

    def whole(ref, here):
        return jnp.concatenate([ref[half, here] for half in range(halves)], axis=1)

    def line(row):
        return whole(cells, pl.ds(row, fields, stride=rows))

    edge[0, 0:fields] = line(0)
    edge[0, fields:2 * fields] = line(1)
    edge[0, 2 * fields:] = jnp.broadcast_to(cover[0:1], (8, columns))
    edge[1, 0:fields] = line(rows - 1)
    edge[1, fields:2 * fields] = line(rows - 2)
    edge[1, 2 * fields:] = jnp.broadcast_to(cover[rows - 1:rows], (8, columns))

    pl.semaphore_wait(barrier, tiles + 2)

    send_lists = pltpu.make_async_remote_copy(
        src_ref=lists_hbm, dst_ref=lists, send_sem=list_send, recv_sem=list_recv,
        device_id=(other, me), device_id_type=MESH,
    )
    send_lists.start()
    send_edges = [
        pltpu.make_async_remote_copy(
            src_ref=edge.at[end], dst_ref=halo.at[end], send_sem=edge_send.at[end],
            recv_sem=edge_recv.at[end], device_id=(comp, neighbour), device_id_type=MESH,
        )
        for end, neighbour in ((0, above), (1, below))
    ]
    for copy in send_edges:
        copy.start()
    send_lists.wait()

    @pl.loop(0, tiles, unroll=tiles)
    def _(step):
        tile = target_tile(me, step, tiles)
        for slot in range(slots):
            outbox[tile, slot] = surface[lists[slot, tile]]
        pltpu.make_async_remote_copy(
            src_ref=outbox.at[tile], dst_ref=inbox.at[pl.ds(me * slots, slots)],
            send_sem=box_send, recv_sem=box_recv.at[me],
            device_id=(other, tile), device_id_type=MESH,
        ).start()

    place = lax.broadcasted_iota(jnp.int32, (slots, tiles), 1) * slots + lax.broadcasted_iota(
        jnp.int32, (slots, tiles), 0
    )

    def find(block, found):
        for source in range(sources):
            found = jnp.where(place == pos_ref[source, block], block * sources + source, found)
        return found

    users_v[...] = lax.fori_loop(0, blocks, find, jnp.zeros((slots, tiles), jnp.int32), unroll=8)
    move_users = pltpu.make_async_copy(users_v, users, users_sem)
    move_users.start()

    for copy in send_edges:
        copy.wait()

    number = lax.broadcasted_iota(jnp.int32, (fields, columns), 0)
    rates = jnp.zeros((fields, columns), jnp.float32)
    for field in range(fields):
        rates = jnp.where(number == field, diffusion_ref[0, field], rates)

    def across(value):
        return pltpu.roll(value, 1, 1) + pltpu.roll(value, columns - 1, 1)

    for end, row in ((1, 0), (0, rows - 1)):
        near, far = halo[end, 0:fields], halo[end, fields:2 * fields]
        total = far + line(row) + across(near) - 4.0 * near
        side[end] = near + rates * halo[end, 2 * fields:2 * fields + 1] * total

    row_number = lax.broadcasted_iota(jnp.int32, (rows, columns), 0)

    def substep(value, first, last, rate):
        up = jnp.where(row_number == 0, first, pltpu.roll(value, 1, 0))
        down = jnp.where(row_number == rows - 1, last, pltpu.roll(value, rows - 1, 0))
        total = up + down + across(value) - 4.0 * value
        return value + rate * cover[...] * total

    @pl.loop(0, fields)
    def _(field):
        here = pl.ds(pl.multiple_of(field * rows, rows), rows)
        rate = diffusion_ref[0, field]
        value = whole(cells, here)
        value = substep(value, halo[1, pl.ds(field, 1)], halo[0, pl.ds(field, 1)], rate)
        value = substep(value, side[1, pl.ds(field, 1)], side[0, pl.ds(field, 1)], rate)
        for half in range(halves):
            stepped[half, here] = value[:, half * BLOCK:(half + 1) * BLOCK]

    move_users.wait()
    load_weights.wait()

    @pl.loop(0, tiles // GROUP)
    def _(group):
        froms = [target_tile(me, group * GROUP + turn, tiles) for turn in range(GROUP)]
        for tile in froms:
            arrived = inbox.at[pl.ds(tile * slots, slots)]
            pltpu.make_async_copy(arrived, arrived, box_recv.at[tile]).wait()
        for tile in froms:
            for slot in range(0, slots, 2):
                first = tile * slots + slot
                nothing = jnp.zeros((fields, BLOCK), jnp.bfloat16)
                picked = jnp.concatenate([
                    jnp.concatenate([inbox[first], nothing], axis=1),
                    jnp.concatenate([nothing, inbox[first + 1]], axis=1),
                ], axis=0)
                weight = jnp.concatenate(
                    [weights[users[slot, tile]], weights[users[slot + 1, tile]]], axis=1
                )
                pair = lax.dot_general(
                    picked, weight, (((1,), (1,)), ((), ())), preferred_element_type=jnp.float32
                )
                products[first] = pair[:fields]
                products[first + 1] = pair[fields:]

    pltpu.make_async_copy(outbox, outbox, box_send).wait()


def finish(
    fields, rows, columns, sources,
    products, stepped, cover, coupling_ref, pos_ref, new_hbm, flux_hbm, new, flux, new_sem, flux_sem,
):
    halves = columns // BLOCK
    copies = []
    for group in range(rows // GROUP_ROWS):
        for half in range(halves):
            totals = []
            for row in range(group * GROUP_ROWS, (group + 1) * GROUP_ROWS):
                block = row * halves + half
                total = products[pos_ref[0, block]]
                for source in range(1, sources):
                    total += products[pos_ref[source, block]]
                totals.append(total)
            turned = jnp.swapaxes(jnp.stack(totals), 0, 1)
            for field in range(fields):
                flux[half, pl.ds(field * rows + group * GROUP_ROWS, GROUP_ROWS)] = turned[field]
        shares = cover[group * GROUP_ROWS:(group + 1) * GROUP_ROWS]
        for field in range(fields):
            lines = pl.ds(field * rows + group * GROUP_ROWS, GROUP_ROWS)
            for half in range(halves):
                share = coupling_ref[0, field] * shares[:, half * BLOCK:(half + 1) * BLOCK]
                new[half, lines] = stepped[half, lines] + share * flux[half, lines]
        here = pl.ds(group * GROUP_ROWS, GROUP_ROWS)
        for number, (source, target, sem) in enumerate(((new, new_hbm, new_sem), (flux, flux_hbm, flux_sem))):
            for half in range(halves):
                copy = pltpu.make_async_copy(
                    source.reshape(halves, fields, rows, BLOCK).at[half, :, here],
                    target.at[:, here, pl.ds(half * BLOCK, BLOCK)],
                    sem.at[group, half],
                )
                copy.start()
                copies.append(copy)
    for copy in copies:
        copy.wait()


def per_device(tiles, state, weights, send_slots, recv_pos, diffusion, coupling, sea_mask):
    _, fields, rows, columns = state.shape
    blocks, sources = recv_pos.shape[1:]
    slots = send_slots.shape[3]
    halves = columns // BLOCK
    vmem, smem, hbm = (pl.BlockSpec(memory_space=m) for m in (pltpu.VMEM, pltpu.SMEM, pltpu.HBM))
    edge_rows = 2 * fields + 8
    dma = pltpu.SemaphoreType.DMA
    operands = (
        state.reshape(fields * rows, columns), weights.reshape(blocks * sources, BLOCK, BLOCK),
        send_slots[0, 0].T, recv_pos[0].T, diffusion, coupling, sea_mask,
    )
    between = pl.pallas_call(
        functools.partial(exchange, tiles, slots, fields, rows, columns, blocks, sources),
        out_shape=(
            pltpu.VMEM((tiles * slots, fields, BLOCK), jnp.float32),
            pltpu.VMEM((halves, fields * rows, BLOCK), jnp.float32),
            pltpu.VMEM((rows, columns), jnp.float32),
            pltpu.SMEM((1, fields), jnp.float32),
            pltpu.SMEM((sources, blocks), jnp.int32),
        ),
        in_specs=[hbm] * 7,
        out_specs=(vmem, vmem, vmem, smem, smem),
        scratch_shapes=[
            pltpu.SMEM((1, fields), jnp.float32),
            pltpu.VMEM((rows, columns), jnp.int32),
            pltpu.VMEM((halves, fields * rows, BLOCK), jnp.float32),
            pltpu.VMEM((blocks * sources, BLOCK, BLOCK), jnp.bfloat16),
            pltpu.VMEM((blocks, fields, BLOCK), jnp.bfloat16),
            pltpu.SMEM((slots, tiles), jnp.int32),
            pltpu.VMEM((tiles, slots, fields, BLOCK), jnp.bfloat16),
            pltpu.VMEM((tiles * slots, fields, BLOCK), jnp.bfloat16),
            pltpu.VMEM((2, edge_rows, columns), jnp.float32),
            pltpu.VMEM((2, edge_rows, columns), jnp.float32),
            pltpu.VMEM((2, fields, columns), jnp.float32),
            pltpu.VMEM((slots, tiles), jnp.int32),
            pltpu.SMEM((slots, tiles), jnp.int32),
            dma((4,)), dma((halves,)), dma, dma, dma((2,)), dma((2,)), dma, dma, dma, dma((tiles,)),
        ],
        compiler_params=pltpu.CompilerParams(
            collective_id=0, has_side_effects=True, vmem_limit_bytes=32 * 2**20
        ),
    )(*(pltpu.with_memory_space_constraint(value, pltpu.HBM) for value in operands))
    result = jax.ShapeDtypeStruct((fields, rows, columns), jnp.float32)
    groups = rows // GROUP_ROWS
    new, flux = pl.pallas_call(
        functools.partial(finish, fields, rows, columns, sources),
        out_shape=(result, result),
        in_specs=[vmem, vmem, vmem, smem, smem],
        out_specs=(hbm, hbm),
        scratch_shapes=[
            pltpu.VMEM((halves, fields * rows, BLOCK), jnp.float32),
            pltpu.VMEM((halves, fields * rows, BLOCK), jnp.float32),
            dma((groups, halves)), dma((groups, halves)),
        ],
        compiler_params=pltpu.CompilerParams(vmem_limit_bytes=32 * 2**20),
    )(*between)
    return new[None], flux[None]


def solution(mesh):
    return jax.shard_map(
        functools.partial(per_device, mesh.shape["tile"]),
        mesh=mesh,
        in_specs=(
            P("comp", None, "tile", None),
            P("comp", "tile", None, None, None),
            P("comp", "tile", None, None),
            P("comp", "tile", None),
            P("comp", None),
            P("comp", None),
            P("tile", None),
        ),
        out_specs=(P("comp", None, "tile", None), P("comp", None, "tile", None)),
        check_vma=False,
    )
```

```python
import functools

import jax
import jax.numpy as jnp
from jax import lax
from jax.experimental import pallas as pl
from jax.experimental.pallas import tpu as pltpu
from jax.sharding import PartitionSpec as P

BLOCK = 128
GROUP = 4
GROUP_ROWS = 8
MESH = pl.DeviceIdType.MESH


def target_tile(me, step, tiles):
    if tiles != 64:
        return lax.rem(me + step, tiles)
    x, turn, part = step % 4, step // 4 % 4, step // 16
    y, z_hi, core = (x + turn) % 4, (x + turn + part) % 2, (part // 2 + x // 2) % 2
    return me ^ (z_hi * 32 + x * 8 + y * 2 + core)


def exchange(
    tiles, slots, fields, rows, columns, blocks, sources,
    state_hbm, weights_hbm, lists_hbm, pos_hbm, diffusion_hbm, coupling_hbm, mask_hbm,
    products, stepped, cover, coupling_ref, pos_ref,
    diffusion_ref, mask_ref, cells, weights, surface, lists, outbox, inbox, edge, halo, side, users_v, users,
    small_sem, state_sem, weights_sem, users_sem, edge_send, edge_recv, list_send, list_recv, box_send, box_recv,
):
    comp, me = lax.axis_index("comp"), lax.axis_index("tile")
    other = 1 - comp
    above, below = (me + tiles - 1) % tiles, (me + 1) % tiles
    halves = columns // BLOCK

    load_state = [
        pltpu.make_async_copy(
            state_hbm.at[:, pl.ds(half * BLOCK, BLOCK)], cells.at[half], state_sem.at[half]
        )
        for half in range(halves)
    ]
    for copy in load_state:
        copy.start()
    load_small = [
        pltpu.make_async_copy(source, target, small_sem.at[number])
        for number, (source, target) in enumerate((
            (pos_hbm, pos_ref), (diffusion_hbm, diffusion_ref),
            (coupling_hbm, coupling_ref), (mask_hbm, mask_ref),
        ))
    ]
    for copy in load_small:
        copy.start()
    load_weights = pltpu.make_async_copy(weights_hbm, weights, weights_sem)
    load_weights.start()

    barrier = pltpu.get_barrier_semaphore()
    for neighbour in (above, below):
        pl.semaphore_signal(barrier, inc=1, device_id=(comp, neighbour), device_id_type=MESH)

    @pl.loop(0, tiles, unroll=tiles)
    def _(step):
        pl.semaphore_signal(
            barrier, inc=1, device_id=(other, target_tile(me, step, tiles)), device_id_type=MESH
        )

    for copy in load_small:
        copy.wait()
    cover[...] = jnp.where(comp == 1, mask_ref[...].astype(jnp.float32), 1.0)
    for copy in load_state:
        copy.wait()

    @pl.loop(0, rows)
    def _(row):
        for half in range(halves):
            picked = cells[half, pl.ds(row, fields, stride=rows)]
            surface[row * halves + half] = picked.astype(jnp.bfloat16)

    def whole(ref, here):
        return jnp.concatenate([ref[half, here] for half in range(halves)], axis=1)

    def line(row):
        return whole(cells, pl.ds(row, fields, stride=rows))

    edge[0, 0:fields] = line(0)
    edge[0, fields:2 * fields] = line(1)
    edge[0, 2 * fields:] = jnp.broadcast_to(cover[0:1], (8, columns))
    edge[1, 0:fields] = line(rows - 1)
    edge[1, fields:2 * fields] = line(rows - 2)
    edge[1, 2 * fields:] = jnp.broadcast_to(cover[rows - 1:rows], (8, columns))

    pl.semaphore_wait(barrier, tiles + 2)

    send_lists = pltpu.make_async_remote_copy(
        src_ref=lists_hbm, dst_ref=lists, send_sem=list_send, recv_sem=list_recv,
        device_id=(other, me), device_id_type=MESH,
    )
    send_lists.start()
    send_edges = [
        pltpu.make_async_remote_copy(
            src_ref=edge.at[end], dst_ref=halo.at[end], send_sem=edge_send.at[end],
            recv_sem=edge_recv.at[end], device_id=(comp, neighbour), device_id_type=MESH,
        )
        for end, neighbour in ((0, above), (1, below))
    ]
    for copy in send_edges:
        copy.start()
    send_lists.wait()

    @pl.loop(0, tiles, unroll=tiles)
    def _(step):
        tile = target_tile(me, step, tiles)
        for slot in range(slots):
            outbox[tile, slot] = surface[lists[slot, tile]]
        pltpu.make_async_remote_copy(
            src_ref=outbox.at[tile], dst_ref=inbox.at[pl.ds(me * slots, slots)],
            send_sem=box_send, recv_sem=box_recv.at[me],
            device_id=(other, tile), device_id_type=MESH,
        ).start()

    place = lax.broadcasted_iota(jnp.int32, (slots, tiles), 1) * slots + lax.broadcasted_iota(
        jnp.int32, (slots, tiles), 0
    )

    def find(block, found):
        for source in range(sources):
            found = jnp.where(place == pos_ref[source, block], block * sources + source, found)
        return found

    users_v[...] = lax.fori_loop(0, blocks, find, jnp.zeros((slots, tiles), jnp.int32), unroll=8)
    move_users = pltpu.make_async_copy(users_v, users, users_sem)
    move_users.start()

    for copy in send_edges:
        copy.wait()

    number = lax.broadcasted_iota(jnp.int32, (fields, columns), 0)
    rates = jnp.zeros((fields, columns), jnp.float32)
    for field in range(fields):
        rates = jnp.where(number == field, diffusion_ref[0, field], rates)

    def across(value):
        return pltpu.roll(value, 1, 1) + pltpu.roll(value, columns - 1, 1)

    for end, row in ((1, 0), (0, rows - 1)):
        near, far = halo[end, 0:fields], halo[end, fields:2 * fields]
        total = far + line(row) + across(near) - 4.0 * near
        side[end] = near + rates * halo[end, 2 * fields:2 * fields + 1] * total

    row_number = lax.broadcasted_iota(jnp.int32, (rows, columns), 0)

    def substep(value, first, last, rate):
        up = jnp.where(row_number == 0, first, pltpu.roll(value, 1, 0))
        down = jnp.where(row_number == rows - 1, last, pltpu.roll(value, rows - 1, 0))
        total = up + down + across(value) - 4.0 * value
        return value + rate * cover[...] * total

    @pl.loop(0, fields)
    def _(field):
        here = pl.ds(pl.multiple_of(field * rows, rows), rows)
        rate = diffusion_ref[0, field]
        value = whole(cells, here)
        value = substep(value, halo[1, pl.ds(field, 1)], halo[0, pl.ds(field, 1)], rate)
        value = substep(value, side[1, pl.ds(field, 1)], side[0, pl.ds(field, 1)], rate)
        for half in range(halves):
            stepped[half, here] = value[:, half * BLOCK:(half + 1) * BLOCK]

    move_users.wait()
    load_weights.wait()

    @pl.loop(0, tiles // GROUP)
    def _(group):
        froms = [target_tile(me, group * GROUP + turn, tiles) for turn in range(GROUP)]
        for tile in froms:
            arrived = inbox.at[pl.ds(tile * slots, slots)]
            pltpu.make_async_copy(arrived, arrived, box_recv.at[tile]).wait()
        for tile in froms:
            for slot in range(0, slots, 2):
                first = tile * slots + slot
                nothing = jnp.zeros((fields, BLOCK), jnp.bfloat16)
                picked = jnp.concatenate([
                    jnp.concatenate([inbox[first], nothing], axis=1),
                    jnp.concatenate([nothing, inbox[first + 1]], axis=1),
                ], axis=0)
                weight = jnp.concatenate(
                    [weights[users[slot, tile]], weights[users[slot + 1, tile]]], axis=1
                )
                pair = lax.dot_general(
                    picked, weight, (((1,), (1,)), ((), ())), preferred_element_type=jnp.float32
                )
                products[first] = pair[:fields]
                products[first + 1] = pair[fields:]

    pltpu.make_async_copy(outbox, outbox, box_send).wait()


def finish(
    fields, rows, columns, sources,
    products, stepped, cover, coupling_ref, pos_ref, new_hbm, flux_hbm, new, flux, new_sem, flux_sem,
):
    halves = columns // BLOCK
    copies = []
    for group in range(rows // GROUP_ROWS):
        for half in range(halves):
            totals = []
            for row in range(group * GROUP_ROWS, (group + 1) * GROUP_ROWS):
                block = row * halves + half
                total = products[pos_ref[0, block]]
                for source in range(1, sources):
                    total += products[pos_ref[source, block]]
                totals.append(total)
            turned = jnp.swapaxes(jnp.stack(totals), 0, 1)
            for field in range(fields):
                flux[half, pl.ds(field * rows + group * GROUP_ROWS, GROUP_ROWS)] = turned[field]
        here = pl.ds(group * GROUP_ROWS, GROUP_ROWS)

        def send(source, target, sem):
            for half in range(halves):
                copy = pltpu.make_async_copy(
                    source.reshape(halves, fields, rows, BLOCK).at[half, :, here],
                    target.at[:, here, pl.ds(half * BLOCK, BLOCK)],
                    sem.at[group, half],
                )
                copy.start()
                copies.append(copy)

        send(flux, flux_hbm, flux_sem)
        shares = cover[group * GROUP_ROWS:(group + 1) * GROUP_ROWS]
        for field in range(fields):
            lines = pl.ds(field * rows + group * GROUP_ROWS, GROUP_ROWS)
            for half in range(halves):
                share = coupling_ref[0, field] * shares[:, half * BLOCK:(half + 1) * BLOCK]
                new[half, lines] = stepped[half, lines] + share * flux[half, lines]
        send(new, new_hbm, new_sem)
    for copy in copies:
        copy.wait()


def per_device(tiles, state, weights, send_slots, recv_pos, diffusion, coupling, sea_mask):
    _, fields, rows, columns = state.shape
    blocks, sources = recv_pos.shape[1:]
    slots = send_slots.shape[3]
    halves = columns // BLOCK
    vmem, smem, hbm = (pl.BlockSpec(memory_space=m) for m in (pltpu.VMEM, pltpu.SMEM, pltpu.HBM))
    edge_rows = 2 * fields + 8
    dma = pltpu.SemaphoreType.DMA
    operands = (
        state.reshape(fields * rows, columns), weights.reshape(blocks * sources, BLOCK, BLOCK),
        send_slots[0, 0].T, recv_pos[0].T, diffusion, coupling, sea_mask,
    )
    between = pl.pallas_call(
        functools.partial(exchange, tiles, slots, fields, rows, columns, blocks, sources),
        out_shape=(
            pltpu.VMEM((tiles * slots, fields, BLOCK), jnp.float32),
            pltpu.VMEM((halves, fields * rows, BLOCK), jnp.float32),
            pltpu.VMEM((rows, columns), jnp.float32),
            pltpu.SMEM((1, fields), jnp.float32),
            pltpu.SMEM((sources, blocks), jnp.int32),
        ),
        in_specs=[hbm] * 7,
        out_specs=(vmem, vmem, vmem, smem, smem),
        scratch_shapes=[
            pltpu.SMEM((1, fields), jnp.float32),
            pltpu.VMEM((rows, columns), jnp.int32),
            pltpu.VMEM((halves, fields * rows, BLOCK), jnp.float32),
            pltpu.VMEM((blocks * sources, BLOCK, BLOCK), jnp.bfloat16),
            pltpu.VMEM((blocks, fields, BLOCK), jnp.bfloat16),
            pltpu.SMEM((slots, tiles), jnp.int32),
            pltpu.VMEM((tiles, slots, fields, BLOCK), jnp.bfloat16),
            pltpu.VMEM((tiles * slots, fields, BLOCK), jnp.bfloat16),
            pltpu.VMEM((2, edge_rows, columns), jnp.float32),
            pltpu.VMEM((2, edge_rows, columns), jnp.float32),
            pltpu.VMEM((2, fields, columns), jnp.float32),
            pltpu.VMEM((slots, tiles), jnp.int32),
            pltpu.SMEM((slots, tiles), jnp.int32),
            dma((4,)), dma((halves,)), dma, dma, dma((2,)), dma((2,)), dma, dma, dma, dma((tiles,)),
        ],
        compiler_params=pltpu.CompilerParams(
            collective_id=0, has_side_effects=True, vmem_limit_bytes=32 * 2**20
        ),
    )(*(pltpu.with_memory_space_constraint(value, pltpu.HBM) for value in operands))
    result = jax.ShapeDtypeStruct((fields, rows, columns), jnp.float32)
    groups = rows // GROUP_ROWS
    new, flux = pl.pallas_call(
        functools.partial(finish, fields, rows, columns, sources),
        out_shape=(result, result),
        in_specs=[vmem, vmem, vmem, smem, smem],
        out_specs=(hbm, hbm),
        scratch_shapes=[
            pltpu.VMEM((halves, fields * rows, BLOCK), jnp.float32),
            pltpu.VMEM((halves, fields * rows, BLOCK), jnp.float32),
            dma((groups, halves)), dma((groups, halves)),
        ],
        compiler_params=pltpu.CompilerParams(vmem_limit_bytes=32 * 2**20),
    )(*between)
    return new[None], flux[None]


def solution(mesh):
    return jax.shard_map(
        functools.partial(per_device, mesh.shape["tile"]),
        mesh=mesh,
        in_specs=(
            P("comp", None, "tile", None),
            P("comp", "tile", None, None, None),
            P("comp", "tile", None, None),
            P("comp", "tile", None),
            P("comp", None),
            P("comp", None),
            P("tile", None),
        ),
        out_specs=(P("comp", None, "tile", None), P("comp", None, "tile", None)),
        check_vma=False,
    )
```
